128 devices in a mesh: expert: 32 (over z, x_lo, y), replica: 4 (over x_hi, core).
Axes of the slice: x: 4 (x_hi: 2, x_lo: 2; x = x_hi * 2 + x_lo), y: 4, z: 4, core: 2. Of those that a mesh axis runs over, the one named last changes fastest.
Arguments:
- out_grad: bfloat16 [4, 4096, 4096], P('replica', 'expert'), may hold values from -2.390625 to 2.390625
- gates: bfloat16 [4, 4096, 8], P('replica', 'expert'), may hold values from 0.049804688 to 0.3984375
- expert_index: int32 [4, 4096, 8], P('replica', 'expert'), may hold values from 0 to 63, as said below
- saved_hidden: bfloat16 [4, 64, 1536, 768], P('replica', 'expert'), may hold values from -0.29882812 to 0.29882812
- down_weight: bfloat16 [64, 768, 4096], P('expert'), may hold values from -0.21875 to 0.21875
Outputs:
- hidden_grad: bfloat16 [4, 64, 1536, 768], P('replica', 'expert')
- gate_grad: float32 [4, 4096, 8], P('replica', 'expert')
- weight_grad: bfloat16 [64, 768, 4096], P('expert', 'replica')
The draws below stay inside these ranges and needn't reach their ends.
Inputs may be any that keep to these rules, and one draw needn't show every extreme that they name: `expert_index`: each token names 8 different experts. Among the 128 tokens of one device no expert is named by more than 48, and the 2 experts of one index of the expert axis together by no more than 75 pairs; in each batch one expert is named by exactly 48 tokens of every device, so it fills all 1536 of its slots, and every device routes exactly 75 pairs to that expert's index of the expert axis.
All inputs are finite; a program needn't handle non-finite values.
Results may differ from the reference program's by a relative error of at most 0.013.
Values may be sent and summed in bfloat16 or wider, within the bound.
No kernel may reach another device: no remote copies, remote signals or barrier semaphores. Data moves between devices by JAX's collectives and lax.ppermute only.
A program may use at most 192 MiB of HBM per device.

```python
import jax
import jax.numpy as jnp
from jax import lax

D = 4096
HID = 768
EXP_DEV = 2
TOP = 8
TOK_DEV = 128
EXPERTS = 64
GROUPS = 4
TOKENS = 4096
MOST = 48
CAP = 1536


def route_block(block_key, hot_expert):
    key_rank = jax.random.fold_in(block_key, 1)
    key_order = jax.random.fold_in(block_key, 2)
    key_place = jax.random.fold_in(block_key, 3)
    ranking = jax.random.permutation(key_rank, TOK_DEV)
    is_hot = ranking < MOST
    needed = TOP - is_hot.astype(jnp.int32)
    begins = jnp.cumsum(needed) - needed
    others = jax.random.permutation(key_order, EXPERTS - 1).astype(jnp.int32)
    others = others + (others >= hot_expert).astype(jnp.int32)
    sibling = hot_expert - hot_expert % EXP_DEV + (hot_expert % EXP_DEV + 1) % EXP_DEV
    sibling_place = jnp.argmax((others == sibling).astype(jnp.int32)).astype(jnp.int32)
    first_entry = others[0]
    others = others.at[sibling_place].set(first_entry).at[0].set(sibling).astype(jnp.int32)
    sequence = jnp.concatenate([others, others[:TOP]])
    length = EXPERTS - 1 + TOP
    hot_place = jax.random.randint(key_place, (TOK_DEV,), 0, TOP)
    column = jnp.arange(TOP, dtype=jnp.int32)
    shifted = (is_hot[:, None] & (column[None, :] > hot_place[:, None])).astype(jnp.int32)
    offsets = column[None, :] - shifted
    chosen = sequence[(begins[:, None] + offsets) % length]
    hot_here = is_hot[:, None] & (column[None, :] == hot_place[:, None])
    return jnp.where(hot_here, hot_expert, chosen).astype(jnp.int32)


def draw_expert_index(key, part):
    key = jax.random.fold_in(key, 11)
    blocks = TOKENS // TOK_DEV
    hot_all = jax.random.randint(jax.random.fold_in(key, 1), (GROUPS,), 0, EXPERTS)
    block_base = jax.random.fold_in(key, 2)

    def per_block(number, hot_expert):
        return route_block(jax.random.fold_in(block_base, number), hot_expert)

    def per_group(group_id, hot_expert):
        numbers = group_id * blocks + jnp.arange(blocks, dtype=jnp.int32)
        return jax.vmap(lambda number: per_block(number, hot_expert))(numbers)
    routed = jax.vmap(per_group)(jnp.arange(GROUPS, dtype=jnp.int32), hot_all)
    return routed.reshape(GROUPS, TOKENS, TOP)


def block_levels(rng, dims, cuts, smallest, high):
    gain = 1.0
    for axis_at, shards_of in cuts:
        draws = jax.random.uniform(jax.random.fold_in(jax.random.fold_in(rng, 6), axis_at), (shards_of,), jnp.float32, smallest / len(cuts), high / len(cuts))
        gain = gain * jnp.repeat(jnp.exp(draws), dims[axis_at] // shards_of).reshape((-1,) + (1,) * (len(dims) - 1 - axis_at))
    return gain


def scatter_about(own_key, extent, scale, bound, shards=(), kind=jnp.bfloat16):
    result = scale * jax.random.normal(own_key, extent, jnp.float32)
    if shards:
        result = result * block_levels(own_key, extent, shards, -0.22, 0.18)
    return jnp.clip(result, -bound, bound).astype(kind)


def setup_inputs(seed: int = 0) -> dict:
    key_of = jax.random.split(jax.random.key(seed), 6)
    return {
        "out_grad": scatter_about(key_of[0], (GROUPS, TOKENS, D), 0.4, 2.390625, ((0, 4), (1, 32))),
        "gates": jnp.clip(0.049804688 + 0.3486328 * jax.random.uniform(key_of[1], (GROUPS, TOKENS, TOP), jnp.float32) ** block_levels(key_of[1], (GROUPS, TOKENS, TOP), ((0, 4), (1, 32)), -0.2, 0.2), 0.049804688, 0.3984375).astype(jnp.bfloat16),
        "expert_index": draw_expert_index(jax.random.fold_in(key_of[5], 71), 0),
        "saved_hidden": scatter_about(key_of[3], (GROUPS, EXPERTS, CAP, HID), 0.05, 0.29882812, ((0, 4), (1, 32))),
        "down_weight": scatter_about(key_of[4], (EXPERTS, HID, D), HID ** -0.5, 0.21875, ((0, 32),)),
    }


def slot_numbers(flat_index):
    onehot = (flat_index[:, None] == jnp.arange(EXPERTS, dtype=jnp.int32)[None, :]).astype(jnp.int32)
    earlier = jnp.cumsum(onehot, axis=0) - onehot
    return jnp.sum(earlier * onehot, axis=1).astype(jnp.int32)


def reference(out_grad, gates, expert_index, saved_hidden, down_weight):
    pair_count = TOKENS * TOP
    flat_index = expert_index.reshape(GROUPS, pair_count).astype(jnp.int32)
    flat_gate = gates.reshape(GROUPS, pair_count)
    slot_table = jnp.stack([slot_numbers(flat_index[group_id]) for group_id in range(GROUPS)])
    source_table = jnp.stack([
        jnp.full((EXPERTS, CAP), pair_count, jnp.int32).at[flat_index[group_id], slot_table[group_id]].set(
            jnp.arange(pair_count, dtype=jnp.int32))
        for group_id in range(GROUPS)])

    def per_expert(expert_id):
        weight = down_weight[expert_id]
        hidden_list = []
        gate_list = []
        summed = jnp.zeros((HID, D), jnp.float32)
        for group_id in range(GROUPS):
            source = source_table[group_id, expert_id]
            present = source < pair_count
            chosen = jnp.minimum(source, pair_count - 1).astype(jnp.int32)
            rows_grad = jnp.where(present[:, None], out_grad[group_id][chosen // TOP], jnp.zeros((), out_grad.dtype))
            rows_gate = jnp.where(present, flat_gate[group_id][chosen], jnp.zeros((), gates.dtype)).astype(jnp.float32)
            upstream = jnp.dot(rows_grad, weight.T, preferred_element_type=jnp.float32)
            hidden_list.append((rows_gate[:, None] * upstream).astype(jnp.bfloat16))
            saved = saved_hidden[group_id, expert_id]
            gate_list.append(jnp.sum(saved.astype(jnp.float32) * upstream, axis=1))
            scaled = (rows_gate[:, None] * rows_grad.astype(jnp.float32)).astype(jnp.bfloat16)
            partial_sum = jnp.dot(saved.T, scaled, preferred_element_type=jnp.float32).astype(jnp.bfloat16)
            summed = summed + lax.optimization_barrier(partial_sum).astype(jnp.float32)
        return jnp.stack(hidden_list), jnp.stack(gate_list), summed.astype(jnp.bfloat16)

    hidden_all, gate_all, weight_grad = lax.map(per_expert, jnp.arange(EXPERTS, dtype=jnp.int32))
    hidden_grad = jnp.transpose(hidden_all, (1, 0, 2, 3))
    gate_grad = jnp.stack([gate_all[flat_index[group_id], group_id, slot_table[group_id]]
                           for group_id in range(GROUPS)]).reshape(GROUPS, TOKENS, TOP)
    return hidden_grad, gate_grad, weight_grad
```

```python
import functools

import jax
import jax.numpy as jnp
from jax import lax
from jax.experimental import pallas as pl
from jax.experimental.pallas import tpu as pltpu
from jax.sharding import PartitionSpec as P

SOURCES = 32
TOK = 128
HID = 768
CAP = 1536
EXP = 2
WIDTH = 4096
WINDOW = 64
STAGES = (1024, 1024, 1024, 1024)
SHARE = HID // 4
VMEM_BIG = 56 * 1024 * 1024

NZ, NX, NY = 4, 2, 4


def index_of(z, x, y):
    return ((z % NZ) * NX + (x % NX)) * NY + (y % NY)


def shift(dz, dx, dy):
    return [
        (index_of(z, x, y), index_of(z + dz, x + dx, y + dy))
        for z in range(NZ)
        for x in range(NX)
        for y in range(NY)
    ]


Y_UP, Y_DOWN = shift(0, 0, 1), shift(0, 0, -1)
Z_UP, Z_DOWN = shift(1, 0, 0), shift(-1, 0, 0)
X_SWAP = shift(0, 1, 0)
CORE_SWAP = [(0, 1), (1, 0), (2, 3), (3, 2)]
XHI_SWAP = [(0, 2), (2, 0), (1, 3), (3, 1)]

RING = (0, -1, 1, 2)


def send(value, pairs):
    return lax.ppermute(value, "expert", pairs)


def after(value, *others):
    return lax.optimization_barrier((value, *others))[0]


def block_order(first_z):
    order = []
    for outer in RING:
        for inner in RING:
            for dx in (0, 1):
                order.append((inner, dx, outer) if first_z else (outer, dx, inner))
    return order


def source_table():
    me = lax.axis_index("expert")
    z, x, y = me // (NX * NY), (me // NY) % NX, me % NY
    tables = []
    for first_z in (True, False):
        moves = jnp.array(block_order(first_z), jnp.int32)
        tables.append(
            (((z + moves[:, 0]) % NZ) * NX + (x + moves[:, 1]) % NX) * NY + (y + moves[:, 2]) % NY
        )
    return jnp.concatenate(tables).astype(jnp.int32)


def one_hot_rows(rel_row):
    rows = lax.broadcasted_iota(jnp.int32, (WINDOW, TOK), 0)
    return rows == rel_row


def prepare_kernel(base_ref, core_ref, rel_ref, gate_ref, saved_ref, scaled_ref, slot_gate_ref, column):
    expert = pl.program_id(0)
    column[...] = jnp.zeros_like(column)

    def add_window(source, carry):
        hit = one_hot_rows(rel_ref[source, pl.ds(expert, 1), :])
        gate = gate_ref[source, pl.ds(expert, 1), :]
        values = jnp.sum(jnp.where(hit, gate, 0.0), axis=1, keepdims=True)
        start = pl.multiple_of(base_ref[source * EXP + expert], 16)
        column[pl.ds(start, WINDOW), :] += jnp.broadcast_to(values, (WINDOW, TOK))
        return carry

    lax.fori_loop(0, SOURCES, add_window, 0)
    slot_gate_ref[0] = column[...]
    core = core_ref[0]
    xhi = core_ref[1]
    step = 256

    def turn(tile, carry):
        rows = pl.ds(pl.multiple_of(tile * step, step), step)
        gate = column[rows, :]
        block = saved_ref[0, 0, rows, :].astype(jnp.float32)
        block = block * jnp.concatenate([gate] * (HID // TOK), axis=1)
        turned = block.T.astype(jnp.bfloat16)
        for owner in range(4):
            owner_xhi, owner_core = owner // 2, owner % 2
            place = jnp.where(core == owner_core, 2, 0) + jnp.where(xhi == owner_xhi, 0, 1)
            start = pl.multiple_of(place * SHARE, SHARE)
            scaled_ref[0, pl.ds(start, SHARE), rows] = turned[owner * SHARE : (owner + 1) * SHARE, :]
        return carry

    lax.fori_loop(0, CAP // step, turn, 0)


def prepare(base, place, rel, gate, saved):
    return pl.pallas_call(
        prepare_kernel,
        grid_spec=pltpu.PrefetchScalarGridSpec(
            num_scalar_prefetch=2,
            grid=(EXP,),
            in_specs=[
                pl.BlockSpec((SOURCES, EXP, TOK), lambda e, *_: (0, 0, 0)),
                pl.BlockSpec((SOURCES, EXP, TOK), lambda e, *_: (0, 0, 0)),
                pl.BlockSpec((1, 1, CAP, HID), lambda e, *_: (0, e, 0, 0)),
            ],
            out_specs=[
                pl.BlockSpec((1, HID, CAP), lambda e, *_: (e, 0, 0)),
                pl.BlockSpec((1, CAP, TOK), lambda e, *_: (e, 0, 0)),
            ],
            scratch_shapes=[pltpu.VMEM((CAP, TOK), jnp.float32)],
        ),
        out_shape=[
            jax.ShapeDtypeStruct((EXP, HID, CAP), jnp.bfloat16),
            jax.ShapeDtypeStruct((EXP, CAP, TOK), jnp.float32),
        ],
        compiler_params=pltpu.CompilerParams(vmem_limit_bytes=40 * 1024 * 1024),
        cost_estimate=pl.CostEstimate(flops=10**9, bytes_accessed=12 * 10**6, transcendentals=0),
        name="prepare",
    )(base, place, rel, gate, saved)


def select_kernel(width, base_ref, order_ref, rel_ref, scaled_ref, *refs):
    pieces = refs[:10]
    rows_ref, go_ref, stay_ref = refs[10:13]
    half = width // 2
    rows_ref[...] = jnp.zeros_like(rows_ref)
    for side in range(2):
        first = side * SOURCES
        columns = slice(side * half, (side + 1) * half)
        for piece in pieces[side * 5 : side * 5 + 5]:
            count = piece.shape[0] // TOK

            def place(number, carry, piece=piece, first=first, columns=columns):
                source = order_ref[first + number]
                hits = [
                    one_hot_rows(rel_ref[source, expert : expert + 1, :]) for expert in range(EXP)
                ]
                pick = jnp.concatenate(hits, axis=0).astype(jnp.float32).astype(jnp.bfloat16)
                start = pl.multiple_of(number * TOK, TOK)
                found = jnp.dot(
                    pick, piece[pl.ds(start, TOK), :], preferred_element_type=jnp.float32
                ).astype(jnp.bfloat16)
                for expert in range(EXP):
                    low = pl.multiple_of(base_ref[source * EXP + expert], 16)
                    rows_ref[expert, pl.ds(low, WINDOW), columns] += found[
                        expert * WINDOW : (expert + 1) * WINDOW
                    ]
                return carry

            lax.fori_loop(0, count, place, 0)
            first += count
    tile = 256
    for expert in range(EXP):

        def multiply(number, carry, expert=expert):
            columns = pl.ds(pl.multiple_of(number * tile, tile), tile)
            product = jnp.dot(
                scaled_ref[expert], rows_ref[expert, :, columns], preferred_element_type=jnp.float32
            ).astype(jnp.bfloat16)
            for part in range(2):
                go_ref[part, expert, :, columns] = product[part * SHARE : (part + 1) * SHARE]
                stay_ref[part, expert, :, columns] = product[(part + 2) * SHARE : (part + 3) * SHARE]
            return carry

        lax.fori_loop(0, width // tile, multiply, 0)


def select(width, base, order, rel, scaled, pieces):
    vmem = pl.BlockSpec(memory_space=pltpu.VMEM)
    smem = pl.BlockSpec(memory_space=pltpu.SMEM)
    return pl.pallas_call(
        functools.partial(select_kernel, width),
        in_specs=[smem, smem, vmem, vmem] + [vmem] * 10,
        out_specs=[vmem, vmem, vmem],
        out_shape=[
            jax.ShapeDtypeStruct((EXP, CAP, width), jnp.bfloat16),
            jax.ShapeDtypeStruct((2, EXP, SHARE, width), jnp.bfloat16),
            jax.ShapeDtypeStruct((2, EXP, SHARE, width), jnp.bfloat16),
        ],
        compiler_params=pltpu.CompilerParams(vmem_limit_bytes=VMEM_BIG),
        cost_estimate=pl.CostEstimate(
            flops=2 * EXP * CAP * HID * width * 2,
            bytes_accessed=SOURCES * TOK * width * 2 + EXP * CAP * width * 2 + 8 * 10**6,
            transcendentals=0,
        ),
        name="select",
    )(base, order, rel, scaled, *pieces)


ROW_TILE = 512


def upstream_kernel(has_total, last, *refs):
    refs = list(refs)
    rows_ref, weight_ref = refs[0], refs[1]
    at = 2
    product = lax.dot_general(
        rows_ref[0], weight_ref[0], (((1,), (1,)), ((), ())), preferred_element_type=jnp.float32
    )
    if has_total:
        product = product + refs[at][0]
        at += 1
    if not last:
        refs[at][0] = product
        return
    saved_ref, gate_ref, hidden_ref, sum_ref = refs[at : at + 4]
    gate = gate_ref[0]
    hidden_ref[0, 0] = (product * jnp.concatenate([gate] * (HID // TOK), axis=1)).astype(jnp.bfloat16)
    sums = jnp.sum(product * saved_ref[0, 0].astype(jnp.float32), axis=1, keepdims=True)
    sum_ref[0] = jnp.broadcast_to(sums, (ROW_TILE, TOK))


def upstream(rows, weight, column_block, total, saved, slot_gate, last):
    width = rows.shape[2]
    in_specs = [
        pl.BlockSpec((1, ROW_TILE, width), lambda e, t: (e, t, 0)),
        pl.BlockSpec((1, HID, width), lambda e, t: (e, 0, column_block)),
    ]
    args = [rows, weight]
    total_spec = pl.BlockSpec((1, ROW_TILE, HID), lambda e, t: (e, t, 0))
    aliases = {}
    if total is not None:
        in_specs.append(total_spec)
        args.append(total)
        if not last:
            aliases = {2: 0}
    if last:
        whole = pl.BlockSpec((1, 1, ROW_TILE, HID), lambda e, t: (0, e, t, 0))
        in_specs += [whole, pl.BlockSpec((1, ROW_TILE, TOK), lambda e, t: (e, t, 0))]
        args += [saved, slot_gate]
        out_specs = [whole, pl.BlockSpec((1, ROW_TILE, TOK), lambda e, t: (e, t, 0))]
        out_shape = [
            jax.ShapeDtypeStruct((1, EXP, CAP, HID), jnp.bfloat16),
            jax.ShapeDtypeStruct((EXP, CAP, TOK), jnp.float32),
        ]
    else:
        out_specs = total_spec
        out_shape = jax.ShapeDtypeStruct((EXP, CAP, HID), jnp.float32)
    return pl.pallas_call(
        functools.partial(upstream_kernel, total is not None, last),
        grid=(EXP, CAP // ROW_TILE),
        in_specs=in_specs,
        out_specs=out_specs,
        out_shape=out_shape,
        input_output_aliases=aliases,
        compiler_params=pltpu.CompilerParams(vmem_limit_bytes=40 * 1024 * 1024),
        cost_estimate=pl.CostEstimate(
            flops=2 * EXP * CAP * HID * width,
            bytes_accessed=EXP * (CAP * width * 2 + HID * width * 2 + CAP * HID * 8),
            transcendentals=0,
        ),
        name="upstream",
    )(*args)


def spread_kernel(base_ref, rel_ref, sum_ref, out_ref):
    def one(source, carry):
        for expert in range(EXP):
            hit = one_hot_rows(rel_ref[source, expert : expert + 1, :])
            low = pl.multiple_of(base_ref[source * EXP + expert], 16)
            values = sum_ref[expert, pl.ds(low, WINDOW), :]
            out_ref[source, expert : expert + 1, :] = jnp.sum(
                jnp.where(hit, values, 0.0), axis=0, keepdims=True
            )
        return carry

    lax.fori_loop(0, SOURCES, one, 0)


def spread(base, rel, sums):
    vmem = pl.BlockSpec(memory_space=pltpu.VMEM)
    smem = pl.BlockSpec(memory_space=pltpu.SMEM)
    return pl.pallas_call(
        spread_kernel,
        in_specs=[smem, vmem, vmem],
        out_specs=vmem,
        out_shape=jax.ShapeDtypeStruct((SOURCES, EXP, TOK), jnp.float32),
        cost_estimate=pl.CostEstimate(flops=10**6, bytes_accessed=2 * 10**6, transcendentals=0),
        name="spread",
    )(base, rel, sums)


def ring_first(block, up, down):
    return send(block, up), send(block, down)


def ring_second(from_up, from_down, up, down):
    half = from_up.shape[0] // 2
    return send(from_up[:half], up), send(from_down[half:], down)


def gate_tables(gates, index):
    index_t = index[0].T
    gates_t = gates[0].T
    experts = jnp.arange(SOURCES * EXP, dtype=jnp.int32)[:, None]
    dense = jnp.zeros((SOURCES * EXP, TOK), jnp.float32)
    for k in range(index_t.shape[0]):
        dense = dense + jnp.where(
            index_t[k][None, :] == experts, gates_t[k][None, :].astype(jnp.float32), 0.0
        )
    dense = dense.astype(jnp.bfloat16).reshape(SOURCES, EXP, TOK)
    gate = lax.all_to_all(dense, "expert", split_axis=0, concat_axis=0, tiled=True)
    present = gate > 0
    ones = present.astype(jnp.float32)
    earlier_token = jnp.triu(jnp.ones((TOK, TOK), jnp.float32), 1)
    rank = jnp.einsum("set,tu->seu", ones, earlier_token, preferred_element_type=jnp.float32)
    counts = jnp.sum(ones, axis=2)
    earlier_source = jnp.tril(jnp.ones((SOURCES, SOURCES), jnp.float32), -1)
    offset = jnp.einsum("rs,se->re", earlier_source, counts, preferred_element_type=jnp.float32)
    offset = offset.astype(jnp.int32)
    base = jnp.minimum(offset // 16 * 16, CAP - WINDOW)
    rel = jnp.where(present, rank.astype(jnp.int32) + (offset - base)[:, :, None], -1)
    return gate.astype(jnp.float32), base.reshape(SOURCES * EXP), rel


def body(out_grad, gates, expert_index, saved_hidden, down_weight):
    tokens = out_grad[0]
    order = source_table()
    replica = lax.axis_index("replica")
    place = jnp.stack([replica % 2, replica // 2]).astype(jnp.int32)

    count = len(STAGES)
    starts = [sum(STAGES[:s]) for s in range(count)]
    own = [tokens[:, starts[s] : starts[s] + STAGES[s]] for s in range(count)]

    gate, base, rel = gate_tables(gates, expert_index)

    def widen(s, hold):
        mine = own[s] if hold is None else after(own[s], *hold)
        both = jnp.concatenate([mine, send(mine, X_SWAP)], axis=0)
        half = STAGES[s] // 2
        a, b = both[:, :half], both[:, half:]
        a_up, a_down = ring_first(a, Z_UP, Z_DOWN)
        b_up, b_down = ring_first(b, Y_UP, Y_DOWN)
        a_far = ring_second(a_up, a_down, Z_UP, Z_DOWN)
        b_far = ring_second(b_up, b_down, Y_UP, Y_DOWN)
        return (
            jnp.concatenate([a, a_up, a_down, *a_far], axis=0),
            jnp.concatenate([b, b_up, b_down, *b_far], axis=0),
        )

    scaled, slot_gate = prepare(base, place, rel, gate, saved_hidden)

    total = None
    shares = []
    hidden_grad = sums = None
    wide = widen(0, None)
    hold = None
    for s in range(count):
        a, b = wide
        if hold is not None:
            a, b = after(a, *hold), after(b, *hold)
        near = (*ring_first(a, Y_UP, Y_DOWN), *ring_first(b, Z_UP, Z_DOWN))
        far_a = ring_second(near[0], near[1], Y_UP, Y_DOWN)
        far_b = ring_second(near[2], near[3], Z_UP, Z_DOWN)
        if s + 1 < count:
            wide = widen(s + 1, (a, b))
        hold = near
        pieces = (a, near[0], near[1], *far_a, b, near[2], near[3], *far_b)
        rows, go, stay = select(STAGES[s], base, order, rel, scaled, pieces)
        met = lax.ppermute(go, "replica", CORE_SWAP)
        pair = (met.astype(jnp.float32) + stay.astype(jnp.float32)).astype(jnp.bfloat16)
        across = lax.ppermute(pair[1], "replica", XHI_SWAP)
        shares.append(
            (pair[0].astype(jnp.float32) + across.astype(jnp.float32)).astype(jnp.bfloat16)
        )
        last = s + 1 == count
        result = upstream(
            rows, down_weight, starts[s] // STAGES[s], total, saved_hidden, slot_gate, last
        )
        if last:
            hidden_grad, sums = result
        else:
            total = result

    weight_grad = jnp.concatenate(shares, axis=2)
    spread_out = spread(base, rel, sums)
    back = lax.all_to_all(spread_out, "expert", split_axis=0, concat_axis=0, tiled=True)
    back = back.reshape(SOURCES * EXP, TOK)
    index_t = expert_index[0].T
    experts = jnp.arange(SOURCES * EXP, dtype=jnp.int32)[None, :, None]
    picked = jnp.sum(jnp.where(index_t[:, None, :] == experts, back[None], 0.0), axis=1)
    gate_grad = picked.T[None]
    return (hidden_grad, gate_grad, weight_grad)


def solution(mesh):
    in_specs = (
        P("replica", "expert", None),
        P("replica", "expert", None),
        P("replica", "expert", None),
        P("replica", "expert", None, None),
        P("expert", None, None),
    )
    out_specs = (
        P("replica", "expert", None, None),
        P("replica", "expert", None),
        P("expert", "replica", None),
    )
    return jax.shard_map(body, mesh=mesh, in_specs=in_specs, out_specs=out_specs, check_vma=False)
```

```python
import functools

import jax
import jax.numpy as jnp
import numpy as np
from jax import lax
from jax.experimental import pallas as pl
from jax.experimental.pallas import tpu as pltpu
from jax.sharding import PartitionSpec as P

SOURCES = 32
TOK = 128
HID = 768
CAP = 1536
EXP = 2
MOST = 48
PICK = EXP * MOST
WINDOW = 64
SHARE = HID // 4
STAGES = (1024, 2048, 1024)
GROUPS = ((0,), (1, 2))
MIB = 1024 * 1024

NZ, NX, NY = 4, 2, 4


def index_of(z, x, y):
    return ((z % NZ) * NX + (x % NX)) * NY + (y % NY)


def shift(dz, dx, dy):
    return [
        (index_of(z, x, y), index_of(z + dz, x + dx, y + dy))
        for z in range(NZ)
        for x in range(NX)
        for y in range(NY)
    ]


Y_UP, Y_DOWN = shift(0, 0, 1), shift(0, 0, -1)
Z_UP, Z_DOWN = shift(1, 0, 0), shift(-1, 0, 0)
X_SWAP = shift(0, 1, 0)
CORE_SWAP = [(0, 1), (1, 0), (2, 3), (3, 2)]
XHI_SWAP = [(0, 2), (2, 0), (1, 3), (3, 1)]

RING = (0, -1, 1, 2)


def send(value, pairs):
    return lax.ppermute(value, "expert", pairs)


def after(value, *others):
    return lax.optimization_barrier((value, *others))[0]


def source_orders():
    table = np.zeros((SOURCES, 2 * SOURCES), np.int32)
    for z in range(NZ):
        for x in range(NX):
            for y in range(NY):
                row = []
                for first_z in (True, False):
                    for outer in RING:
                        for inner in RING:
                            for dx in range(NX):
                                dz, dy = (inner, outer) if first_z else (outer, inner)
                                row.append(index_of(z + dz, x + dx, y + dy))
                table[index_of(z, x, y)] = row
    return table


def prepare_kernel(
    base_ref, lead_ref, count_ref, place_ref, rank_ref, gate_ref, saved_ref,
    scaled_ref, padded_ref, row_gate_ref, pick_ref, moved,
):
    expert = pl.program_id(0)

    def one(source, carry):
        rank = rank_ref[source, pl.ds(expert, 1), :]
        gate = gate_ref[source, pl.ds(expert, 1), :]
        at = source * EXP + expert
        rows = pl.ds(pl.multiple_of(source * MOST, MOST), MOST)
        hit = lax.broadcasted_iota(jnp.int32, (MOST, TOK), 0) == rank
        pick_ref[0, rows, :] = jnp.where(hit, 1.0, 0.0).astype(jnp.bfloat16)
        row_gate = jnp.sum(jnp.where(hit, gate, 0.0), axis=1, keepdims=True)
        row_gate_ref[0, rows, :] = jnp.broadcast_to(row_gate, (MOST, TOK))
        window = saved_ref[0, 0, pl.ds(pl.multiple_of(base_ref[at], 16), WINDOW), :]
        row = lax.broadcasted_iota(jnp.int32, (MOST, WINDOW), 0)
        column = lax.broadcasted_iota(jnp.int32, (MOST, WINDOW), 1)
        take = (column == row + lead_ref[at]) & (row < count_ref[at])
        found = jnp.dot(
            jnp.where(take, 1.0, 0.0).astype(jnp.bfloat16), window,
            preferred_element_type=jnp.float32,
        )
        padded_ref[0, rows, :] = found.astype(jnp.bfloat16)
        moved[rows, :] = found * row_gate
        return carry

    lax.fori_loop(0, SOURCES, one, 0)
    core, xhi = place_ref[0], place_ref[1]
    step = 256

    def turn(tile, carry):
        rows = pl.ds(pl.multiple_of(tile * step, step), step)
        turned = moved[rows, :].T.astype(jnp.bfloat16)
        for owner in range(4):
            owner_xhi, owner_core = owner // 2, owner % 2
            block = jnp.where(core == owner_core, 2, 0) + jnp.where(xhi == owner_xhi, 0, 1)
            start = pl.multiple_of(block * SHARE, SHARE)
            scaled_ref[0, pl.ds(start, SHARE), rows] = turned[owner * SHARE : (owner + 1) * SHARE, :]
        return carry

    lax.fori_loop(0, CAP // step, turn, 0)


def prepare(base, lead, count, place, rank, gate, saved):
    table = pl.BlockSpec((SOURCES, EXP, TOK), lambda e, *_: (0, 0, 0))
    return pl.pallas_call(
        prepare_kernel,
        grid_spec=pltpu.PrefetchScalarGridSpec(
            num_scalar_prefetch=4,
            grid=(EXP,),
            in_specs=[table, table, pl.BlockSpec((1, 1, CAP, HID), lambda e, *_: (0, e, 0, 0))],
            out_specs=[
                pl.BlockSpec((1, HID, CAP), lambda e, *_: (e, 0, 0)),
                pl.BlockSpec((1, CAP, HID), lambda e, *_: (e, 0, 0)),
                pl.BlockSpec((1, CAP, TOK), lambda e, *_: (e, 0, 0)),
                pl.BlockSpec((1, CAP, TOK), lambda e, *_: (e, 0, 0)),
            ],
            scratch_shapes=[pltpu.VMEM((CAP, HID), jnp.float32)],
        ),
        out_shape=[
            jax.ShapeDtypeStruct((EXP, HID, CAP), jnp.bfloat16),
            jax.ShapeDtypeStruct((EXP, CAP, HID), jnp.bfloat16),
            jax.ShapeDtypeStruct((EXP, CAP, TOK), jnp.float32),
            jax.ShapeDtypeStruct((EXP, CAP, TOK), jnp.bfloat16),
        ],
        compiler_params=pltpu.CompilerParams(vmem_limit_bytes=36 * MIB),
        cost_estimate=pl.CostEstimate(flops=10**9, bytes_accessed=16 * 10**6, transcendentals=0),
        name="prepare",
    )(base, lead, count, place, rank, gate, saved)


def join_kernel(*refs):
    pieces, outs, sems = refs[:10], refs[10:12], refs[12]
    copies = []
    for side in range(2):
        first = 0
        for number in range(5):
            piece = pieces[side * 5 + number]
            size = piece.shape[0]
            copy = pltpu.make_async_copy(
                piece, outs[side].at[pl.ds(first, size), :], sems.at[side * 5 + number]
            )
            copy.start()
            copies.append(copy)
            first += size
    for copy in copies:
        copy.wait()


def join(pieces):
    width = pieces[0].shape[1]
    anywhere = pl.BlockSpec(memory_space=pl.ANY)
    shape = jax.ShapeDtypeStruct((1024, width), jnp.bfloat16)
    return pl.pallas_call(
        join_kernel,
        in_specs=[anywhere] * 10,
        out_specs=[anywhere] * 2,
        out_shape=[shape] * 2,
        scratch_shapes=[pltpu.SemaphoreType.DMA((10,))],
        cost_estimate=pl.CostEstimate(
            flops=0, bytes_accessed=2 * 2 * 1024 * width * 2, transcendentals=0
        ),
        name="join",
    )(*pieces)


def select_kernel(width, order_ref, pick_ref, scaled_hbm, *refs):
    pieces = refs[:10]
    rows_out, go_out, stay_out = refs[10:13]
    taken, rows, scaled, go, stay, in_sems, out_sems = refs[13:]
    half = width // 2
    copies = []
    for side in range(2):
        first = 0
        for number in range(5):
            piece = pieces[side * 5 + number]
            size = piece.shape[0]
            copy = pltpu.make_async_copy(
                piece, taken.at[side, pl.ds(first, size), :], in_sems.at[side * 5 + number]
            )
            copy.start()
            copies.append((copy, first, size))
            first += size
    load = pltpu.make_async_copy(scaled_hbm, scaled, in_sems.at[10])
    load.start()

    for side in range(2):
        for number in range(5):
            copy, first, size = copies[side * 5 + number]
            copy.wait()

            def place(block, carry, side=side, first=first):
                at = first // TOK + block
                source = order_ref[side * SOURCES + at]
                to = pl.ds(pl.multiple_of(source * MOST, MOST), MOST)
                pick = jnp.concatenate([pick_ref[e, to, :] for e in range(EXP)], axis=0)
                start = pl.multiple_of(at * TOK, TOK)
                found = jnp.dot(
                    pick, taken[side, pl.ds(start, TOK), :], preferred_element_type=jnp.float32
                ).astype(jnp.bfloat16)
                for e in range(EXP):
                    rows[e, to, side * half : (side + 1) * half] = found[e * MOST : (e + 1) * MOST]
                return carry

            lax.fori_loop(0, size // TOK, place, 0, unroll=2)
    outs = []
    for e in range(EXP):
        copy = pltpu.make_async_copy(rows.at[e], rows_out.at[e], out_sems.at[e])
        copy.start()
        outs.append(copy)
    load.wait()
    tile = 256
    for e in range(EXP):

        def multiply(number, carry, e=e):
            columns = pl.ds(pl.multiple_of(number * tile, tile), tile)
            product = jnp.dot(
                scaled[e], rows[e, :, columns], preferred_element_type=jnp.float32
            ).astype(jnp.bfloat16)
            for part in range(2):
                go[e, part, :, columns] = product[part * SHARE : (part + 1) * SHARE]
                stay[e, part, :, columns] = product[(part + 2) * SHARE : (part + 3) * SHARE]
            return carry

        lax.fori_loop(0, width // tile, multiply, 0)
        for part in range(2):
            for kind, (source, target) in enumerate(((go, go_out), (stay, stay_out))):
                copy = pltpu.make_async_copy(
                    source.at[e, part], target.at[part, e], out_sems.at[2 + (e * 2 + part) * 2 + kind]
                )
                copy.start()
                outs.append(copy)
    for copy in outs:
        copy.wait()


def select(order, pick, scaled, pieces):
    half = pieces[0].shape[1]
    width = 2 * half
    anywhere = pl.BlockSpec(memory_space=pl.ANY)
    vmem = pl.BlockSpec(memory_space=pltpu.VMEM)
    smem = pl.BlockSpec(memory_space=pltpu.SMEM)
    shared = (EXP, 2, SHARE, width)
    need = (2 * SOURCES * TOK * half + EXP * CAP * width + EXP * HID * CAP + 2 * EXP * HID * width // 2) * 2
    return pl.pallas_call(
        functools.partial(select_kernel, width),
        in_specs=[smem, vmem, anywhere] + [anywhere] * 10,
        out_specs=[anywhere] * 3,
        out_shape=[
            jax.ShapeDtypeStruct((EXP, CAP, width), jnp.bfloat16),
            jax.ShapeDtypeStruct((2, EXP, SHARE, width), jnp.bfloat16),
            jax.ShapeDtypeStruct((2, EXP, SHARE, width), jnp.bfloat16),
        ],
        scratch_shapes=[
            pltpu.VMEM((2, SOURCES * TOK, half), jnp.bfloat16),
            pltpu.VMEM((EXP, CAP, width), jnp.bfloat16),
            pltpu.VMEM((EXP, HID, CAP), jnp.bfloat16),
            pltpu.VMEM(shared, jnp.bfloat16),
            pltpu.VMEM(shared, jnp.bfloat16),
            pltpu.SemaphoreType.DMA((11,)),
            pltpu.SemaphoreType.DMA((10,)),
        ],
        compiler_params=pltpu.CompilerParams(vmem_limit_bytes=need + 8 * MIB),
        cost_estimate=pl.CostEstimate(
            flops=2 * EXP * CAP * HID * width * 2,
            bytes_accessed=SOURCES * TOK * width * 2 + EXP * CAP * width * 2 + 8 * 10**6,
            transcendentals=0,
        ),
        name="select",
    )(order, pick, scaled, *pieces)


ROW_TILE = 512
DEPTH = 1024


def upstream_kernel(has_total, last, *refs):
    refs = list(refs)
    rows_ref, weight_ref = refs[0], refs[1]
    product = lax.dot_general(
        rows_ref[0], weight_ref[0], (((1,), (1,)), ((), ())), preferred_element_type=jnp.float32
    )
    at = 2
    if has_total:
        total_ref = refs[at]
        at += 1
    if not last:
        out_ref = refs[at]
        step = pl.program_id(2)

        @pl.when(step == 0)
        def _():
            out_ref[0] = product + total_ref[0] if has_total else product

        @pl.when(step > 0)
        def _():
            out_ref[0] += product

        return
    product = product + total_ref[0]
    padded_ref, gate_ref, pick_ref, hidden_ref, sum_ref = refs[at : at + 5]
    gate = gate_ref[0]
    hidden_ref[0] = (product * jnp.concatenate([gate] * (HID // TOK), axis=1)).astype(jnp.bfloat16)
    sums = jnp.sum(product * padded_ref[0].astype(jnp.float32), axis=1, keepdims=True)
    spread = jnp.where(pick_ref[0].astype(jnp.float32) > 0, sums, 0.0)
    sum_ref[0] = jnp.sum(spread.reshape(ROW_TILE_LAST // MOST, MOST, TOK), axis=1)


ROW_TILE_LAST = 384


def upstream(rows, weight, first_column, total, extra, last):
    width = rows.shape[2]
    depth = DEPTH
    tile = ROW_TILE_LAST if last else ROW_TILE
    steps = width // depth
    assert not last or steps == 1
    lead = first_column // depth
    in_specs = [
        pl.BlockSpec((1, tile, depth), lambda e, t, k: (e, t, k)),
        pl.BlockSpec((1, HID, depth), lambda e, t, k: (e, 0, lead + k)),
    ]
    args = [rows, weight]
    total_spec = pl.BlockSpec((1, tile, HID), lambda e, t, k: (e, t, 0))
    narrow = pl.BlockSpec((1, tile, TOK), lambda e, t, k: (e, t, 0))
    aliases = {}
    if total is not None:
        in_specs.append(total_spec)
        args.append(total)
        if not last:
            aliases = {2: 0}
    if last:
        in_specs += [total_spec, narrow, narrow]
        args += list(extra)
        out_specs = [
            total_spec,
            pl.BlockSpec((1, tile // MOST, TOK), lambda e, t, k: (e, t, 0)),
        ]
        out_shape = [
            jax.ShapeDtypeStruct((EXP, CAP, HID), jnp.bfloat16),
            jax.ShapeDtypeStruct((EXP, SOURCES, TOK), jnp.float32),
        ]
    else:
        out_specs = total_spec
        out_shape = jax.ShapeDtypeStruct((EXP, CAP, HID), jnp.float32)
    return pl.pallas_call(
        functools.partial(upstream_kernel, total is not None, last),
        grid=(EXP, CAP // tile, steps),
        in_specs=in_specs,
        out_specs=out_specs,
        out_shape=out_shape,
        input_output_aliases=aliases,
        compiler_params=pltpu.CompilerParams(vmem_limit_bytes=32 * MIB),
        cost_estimate=pl.CostEstimate(
            flops=2 * EXP * CAP * HID * width // 64,
            bytes_accessed=EXP * CAP * HID,
            transcendentals=0,
        ),
        name="finish" if last else "upstream",
    )(*args)


def order_kernel(base_ref, lead_ref, count_ref, hidden_ref, out_ref):
    expert = pl.program_id(0)
    out_ref[...] = jnp.zeros_like(out_ref)

    def one(source, carry):
        at = source * EXP + expert
        column = lax.broadcasted_iota(jnp.int32, (WINDOW, MOST), 1)
        row = lax.broadcasted_iota(jnp.int32, (WINDOW, MOST), 0)
        take = (row == column + lead_ref[at]) & (column < count_ref[at])
        found = jnp.dot(
            jnp.where(take, 1.0, 0.0).astype(jnp.bfloat16),
            hidden_ref[0, pl.ds(pl.multiple_of(source * MOST, MOST), MOST), :],
            preferred_element_type=jnp.float32,
        ).astype(jnp.bfloat16)
        low = pl.multiple_of(base_ref[at], 16)
        out_ref[0, 0, pl.ds(low, WINDOW), :] += found
        return carry

    lax.fori_loop(0, SOURCES, one, 0, unroll=2)


def in_slot_order(base, lead, count, hidden):
    return pl.pallas_call(
        order_kernel,
        grid_spec=pltpu.PrefetchScalarGridSpec(
            num_scalar_prefetch=3,
            grid=(EXP,),
            in_specs=[pl.BlockSpec((1, CAP, HID), lambda e, *_: (e, 0, 0))],
            out_specs=pl.BlockSpec((1, 1, CAP, HID), lambda e, *_: (0, e, 0, 0)),
        ),
        out_shape=jax.ShapeDtypeStruct((1, EXP, CAP, HID), jnp.bfloat16),
        compiler_params=pltpu.CompilerParams(vmem_limit_bytes=24 * MIB),
        cost_estimate=pl.CostEstimate(flops=10**9, bytes_accessed=12 * 10**6, transcendentals=0),
        name="in_slot_order",
    )(base, lead, count, hidden)


def ring_first(block, up, down):
    return send(block, up), send(block, down)


def ring_second(from_up, from_down, up, down):
    half = from_up.shape[0] // 2
    return send(from_up[:half], up), send(from_down[half:], down)


def gate_tables(gates, index):
    index_t = index[0].T
    gates_t = gates[0].T
    experts = jnp.arange(SOURCES * EXP, dtype=jnp.int32)[None, :, None]
    dense = jnp.sum(
        jnp.where(index_t[:, None, :] == experts, gates_t[:, None, :].astype(jnp.float32), 0.0), axis=0
    )
    dense = dense.astype(jnp.bfloat16).reshape(SOURCES, EXP, TOK)
    gate = lax.all_to_all(dense, "expert", split_axis=0, concat_axis=0, tiled=True)
    present = gate > 0
    ones = present.astype(jnp.float32)
    earlier_token = jnp.triu(jnp.ones((TOK, TOK), jnp.float32), 1)
    rank = jnp.einsum("set,tu->seu", ones, earlier_token, preferred_element_type=jnp.float32)
    counts = jnp.sum(ones, axis=2)
    earlier_source = jnp.tril(jnp.ones((SOURCES, SOURCES), jnp.float32), -1)
    offset = jnp.einsum("rs,se->re", earlier_source, counts, preferred_element_type=jnp.float32)
    offset = offset.astype(jnp.int32)
    base = jnp.minimum(offset // 16 * 16, CAP - WINDOW)
    rank = jnp.where(present, rank.astype(jnp.int32), -1)
    flat = (SOURCES * EXP,)
    return (
        gate.astype(jnp.float32),
        rank,
        base.reshape(flat),
        (offset - base).reshape(flat),
        counts.astype(jnp.int32).reshape(flat),
    )


def body(out_grad, gates, expert_index, saved_hidden, down_weight):
    tokens = out_grad[0]
    order = lax.dynamic_index_in_dim(
        jnp.asarray(source_orders()), lax.axis_index("expert"), 0, keepdims=False
    )
    replica = lax.axis_index("replica")
    place = jnp.stack([replica % 2, replica // 2]).astype(jnp.int32)

    count = len(STAGES)
    starts = [sum(STAGES[:s]) for s in range(count)]

    def first_rings(group, hold, ready):
        lefts, rights, spans = [], [], []
        at = 0
        for s in group:
            half = STAGES[s] // 2
            lefts.append(tokens[:, starts[s] : starts[s] + half])
            rights.append(tokens[:, starts[s] + half : starts[s] + 2 * half])
            spans.append((at, at + half))
            at += half
        mine = jnp.concatenate(lefts + rights, axis=1)
        if hold is not None:
            mine = after(mine, *hold)
        both = jnp.concatenate([mine, send(mine, X_SWAP)], axis=0)
        if ready is not None:
            both = after(both, ready)
        a, b = both[:, :at], both[:, at:]
        a_up, a_down = ring_first(a, Z_UP, Z_DOWN)
        b_up, b_down = ring_first(b, Y_UP, Y_DOWN)
        a_far = ring_second(a_up, a_down, Z_UP, Z_DOWN)
        b_far = ring_second(b_up, b_down, Y_UP, Y_DOWN)
        pieces = (a, a_up, a_down, *a_far, b, b_up, b_down, *b_far)
        if len(group) == 1:
            return {group[0]: join(pieces)}
        return {
            s: join(tuple(piece[:, low:high] for piece in pieces))
            for s, (low, high) in zip(group, spans)
        }

    gate, rank, base, lead, counts = gate_tables(gates, expert_index)
    scaled, padded, row_gate, pick = prepare(base, lead, counts, place, rank, gate, saved_hidden)

    wide = first_rings(GROUPS[0], None, None)
    later = list(GROUPS[1:])
    total = None
    shares = []
    near = pair = None
    selected, crossed = [], []
    hidden = sums = None

    def second_ring_first(s):
        a, b = wide[s]
        hold = list(near or ())
        if s >= 2:
            hold.append(selected[s - 2])
        if hold:
            a, b = after(a, *hold), after(b, *hold)
        return (a, b), (*ring_first(a, Y_UP, Y_DOWN), *ring_first(b, Z_UP, Z_DOWN))

    def second_ring_second(near, hold):
        ends = [after(value, *hold) if hold else value for value in near]
        return (
            ring_second(ends[0], ends[1], Y_UP, Y_DOWN),
            ring_second(ends[2], ends[3], Z_UP, Z_DOWN),
        )

    (a, b), near = second_ring_first(0)
    wide.update(first_rings(later.pop(0), (a, b), scaled))
    far_a, far_b = second_ring_second(near, ())
    for s in range(count):
        pieces = (a, near[0], near[1], *far_a, b, near[2], near[3], *far_b)
        last = s + 1 == count
        if not last:
            (a, b), near = second_ring_first(s + 1)
        hold = []
        if s > 0:
            hold += [total, pair]
        if s > 1:
            hold.append(crossed[s - 2])
        if s + 1 < count:
            hold += [a, b]
        if hold:
            pieces = tuple(after(piece, *hold) for piece in pieces)
        rows, go, stay = select(order, pick, scaled, pieces)
        selected.append(go)
        leaving = after(go, *near) if 0 < s < count - 1 else go
        met = lax.ppermute(leaving, "replica", CORE_SWAP)
        pair = (met.astype(jnp.float32) + stay.astype(jnp.float32)).astype(jnp.bfloat16)
        across = lax.ppermute(pair[1], "replica", XHI_SWAP)
        shares.append(
            (pair[0].astype(jnp.float32) + across.astype(jnp.float32)).astype(jnp.bfloat16)
        )
        if not last:
            far_a, far_b = second_ring_second(near, (go,))
        if last:
            rows = after(rows, pair, *crossed[s - 1 :])
        crossed.append(across)
        result = upstream(rows, down_weight, starts[s], total, (padded, row_gate, pick), last)
        if last:
            hidden, sums = result
        else:
            total = result

    weight_grad = jnp.concatenate(shares, axis=2)
    back = lax.all_to_all(
        jnp.swapaxes(sums, 0, 1), "expert", split_axis=0, concat_axis=0, tiled=True
    ).reshape(SOURCES * EXP, TOK)
    hidden_grad = in_slot_order(base, lead, counts, hidden)
    index_t = expert_index[0].T
    experts = jnp.arange(SOURCES * EXP, dtype=jnp.int32)[None, :, None]
    picked = jnp.sum(jnp.where(index_t[:, None, :] == experts, back[None], 0.0), axis=1)
    gate_grad = picked.T[None]
    return (hidden_grad, gate_grad, weight_grad)


def solution(mesh):
    in_specs = (
        P("replica", "expert", None),
        P("replica", "expert", None),
        P("replica", "expert", None),
        P("replica", "expert", None, None),
        P("expert", None, None),
    )
    out_specs = (
        P("replica", "expert", None, None),
        P("replica", "expert", None),
        P("expert", "replica", None),
    )
    return jax.shard_map(body, mesh=mesh, in_specs=in_specs, out_specs=out_specs, check_vma=False)
```

```python
import functools

import jax
import jax.numpy as jnp
import numpy as np
from jax import lax
from jax.experimental import pallas as pl
from jax.experimental.pallas import tpu as pltpu
from jax.sharding import PartitionSpec as P

SOURCES = 32
TOK = 128
HID = 768
CAP = 1536
EXP = 2
MOST = 48
PICK = EXP * MOST
WINDOW = 64
SHARE = HID // 4
STAGES = (1280, 1536, 1280)
GROUPS = ((0,), (1, 2))
MIB = 1024 * 1024
CROSSED_LAG = 1

NZ, NX, NY = 4, 2, 4


def index_of(z, x, y):
    return ((z % NZ) * NX + (x % NX)) * NY + (y % NY)


def shift(dz, dx, dy):
    return [
        (index_of(z, x, y), index_of(z + dz, x + dx, y + dy))
        for z in range(NZ)
        for x in range(NX)
        for y in range(NY)
    ]


Y_UP, Y_DOWN = shift(0, 0, 1), shift(0, 0, -1)
Z_UP, Z_DOWN = shift(1, 0, 0), shift(-1, 0, 0)
X_SWAP = shift(0, 1, 0)
CORE_SWAP = [(0, 1), (1, 0), (2, 3), (3, 2)]
XHI_SWAP = [(0, 2), (2, 0), (1, 3), (3, 1)]

RING = (0, -1, 1, 2)


def send(value, pairs):
    return lax.ppermute(value, "expert", pairs)


def after(value, *others):
    return lax.optimization_barrier((value, *others))[0]


def source_orders():
    table = np.zeros((SOURCES, 2 * SOURCES), np.int32)
    for z in range(NZ):
        for x in range(NX):
            for y in range(NY):
                row = []
                for first_z in (True, False):
                    for outer in RING:
                        for inner in RING:
                            for dx in range(NX):
                                dz, dy = (inner, outer) if first_z else (outer, inner)
                                row.append(index_of(z + dz, x + dx, y + dy))
                table[index_of(z, x, y)] = row
    return table


def prepare_kernel(
    base_ref, lead_ref, count_ref, place_ref, rank_ref, gate_ref, saved_ref,
    scaled_ref, padded_ref, row_gate_ref, pick_ref, moved,
):
    expert = pl.program_id(0)

    def one(source, carry):
        rank = rank_ref[source, pl.ds(expert, 1), :]
        gate = gate_ref[source, pl.ds(expert, 1), :]
        at = source * EXP + expert
        rows = pl.ds(pl.multiple_of(source * MOST, MOST), MOST)
        hit = lax.broadcasted_iota(jnp.int32, (MOST, TOK), 0) == rank
        pick_ref[0, rows, :] = jnp.where(hit, 1.0, 0.0).astype(jnp.bfloat16)
        row_gate = jnp.sum(jnp.where(hit, gate, 0.0), axis=1, keepdims=True)
        row_gate_ref[0, rows, :] = jnp.broadcast_to(row_gate, (MOST, TOK))
        window = saved_ref[0, 0, pl.ds(pl.multiple_of(base_ref[at], 16), WINDOW), :]
        row = lax.broadcasted_iota(jnp.int32, (MOST, WINDOW), 0)
        column = lax.broadcasted_iota(jnp.int32, (MOST, WINDOW), 1)
        take = (column == row + lead_ref[at]) & (row < count_ref[at])
        found = jnp.dot(
            jnp.where(take, 1.0, 0.0).astype(jnp.bfloat16), window,
            preferred_element_type=jnp.float32,
        )
        padded_ref[0, rows, :] = found.astype(jnp.bfloat16)
        moved[rows, :] = found * row_gate
        return carry

    lax.fori_loop(0, SOURCES, one, 0)
    core, xhi = place_ref[0], place_ref[1]
    step = 256

    def turn(tile, carry):
        rows = pl.ds(pl.multiple_of(tile * step, step), step)
        turned = moved[rows, :].T.astype(jnp.bfloat16)
        for owner in range(4):
            owner_xhi, owner_core = owner // 2, owner % 2
            block = jnp.where(core == owner_core, 2, 0) + jnp.where(xhi == owner_xhi, 0, 1)
            start = pl.multiple_of(block * SHARE, SHARE)
            scaled_ref[0, pl.ds(start, SHARE), rows] = turned[owner * SHARE : (owner + 1) * SHARE, :]
        return carry

    lax.fori_loop(0, CAP // step, turn, 0)


def prepare(base, lead, count, place, rank, gate, saved):
    table = pl.BlockSpec((SOURCES, EXP, TOK), lambda e, *_: (0, 0, 0))
    return pl.pallas_call(
        prepare_kernel,
        grid_spec=pltpu.PrefetchScalarGridSpec(
            num_scalar_prefetch=4,
            grid=(EXP,),
            in_specs=[table, table, pl.BlockSpec((1, 1, CAP, HID), lambda e, *_: (0, e, 0, 0))],
            out_specs=[
                pl.BlockSpec((1, HID, CAP), lambda e, *_: (e, 0, 0)),
                pl.BlockSpec((1, CAP, HID), lambda e, *_: (e, 0, 0)),
                pl.BlockSpec((1, CAP, TOK), lambda e, *_: (e, 0, 0)),
                pl.BlockSpec((1, CAP, TOK), lambda e, *_: (e, 0, 0)),
            ],
            scratch_shapes=[pltpu.VMEM((CAP, HID), jnp.float32)],
        ),
        out_shape=[
            jax.ShapeDtypeStruct((EXP, HID, CAP), jnp.bfloat16),
            jax.ShapeDtypeStruct((EXP, CAP, HID), jnp.bfloat16),
            jax.ShapeDtypeStruct((EXP, CAP, TOK), jnp.float32),
            jax.ShapeDtypeStruct((EXP, CAP, TOK), jnp.bfloat16),
        ],
        compiler_params=pltpu.CompilerParams(vmem_limit_bytes=36 * MIB),
        cost_estimate=pl.CostEstimate(flops=10**9, bytes_accessed=16 * 10**6, transcendentals=0),
        name="prepare",
    )(base, lead, count, place, rank, gate, saved)


def join_kernel(spans, *refs):
    pieces, outs, sems = refs[:10], refs[10:-1], refs[-1]
    copies = []
    for number, (low, high) in enumerate(spans):
        for side in range(2):
            first = 0
            for part in range(5):
                piece = pieces[side * 5 + part]
                size = piece.shape[0]
                copy = pltpu.make_async_copy(
                    piece.at[:, pl.ds(low, high - low)],
                    outs[number * 2 + side].at[pl.ds(first, size), :],
                    sems.at[len(copies)],
                )
                copy.start()
                copies.append(copy)
                first += size
    for copy in copies:
        copy.wait()


def join(pieces, spans):
    shapes = []
    for low, high in spans:
        shapes += [jax.ShapeDtypeStruct((1024, high - low), jnp.bfloat16)] * 2
    return pl.pallas_call(
        functools.partial(join_kernel, spans),
        in_specs=[pl.BlockSpec(memory_space=pl.ANY)] * 10,
        out_specs=[pl.BlockSpec(memory_space=pltpu.VMEM)] * len(shapes),
        out_shape=shapes,
        scratch_shapes=[pltpu.SemaphoreType.DMA((10 * len(spans),))],
        compiler_params=pltpu.CompilerParams(vmem_limit_bytes=16 * MIB),
        cost_estimate=pl.CostEstimate(flops=0, bytes_accessed=2 * MIB, transcendentals=0),
        name="join",
    )(*pieces)


def select_kernel(width, order_ref, pick_ref, scaled_hbm, *refs):
    pieces = refs[:10]
    rows_out, go_out, stay_out = refs[10:13]
    taken, rows, scaled, go, stay, in_sems, out_sems = refs[13:]
    half = width // 2
    copies = []
    for side in range(2):
        first = 0
        for number in range(5):
            piece = pieces[side * 5 + number]
            size = piece.shape[0]
            copy = pltpu.make_async_copy(
                piece, taken.at[side, pl.ds(first, size), :], in_sems.at[side * 5 + number]
            )
            copy.start()
            copies.append((copy, first, size))
            first += size
    load = pltpu.make_async_copy(scaled_hbm, scaled, in_sems.at[10])
    load.start()

    for side in range(2):
        for number in range(5):
            copy, first, size = copies[side * 5 + number]
            copy.wait()

            def place(block, carry, side=side, first=first):
                at = first // TOK + block
                source = order_ref[side * SOURCES + at]
                to = pl.ds(pl.multiple_of(source * MOST, MOST), MOST)
                pick = jnp.concatenate([pick_ref[e, to, :] for e in range(EXP)], axis=0)
                start = pl.multiple_of(at * TOK, TOK)
                found = jnp.dot(
                    pick, taken[side, pl.ds(start, TOK), :], preferred_element_type=jnp.float32
                ).astype(jnp.bfloat16)
                for e in range(EXP):
                    rows[e, to, side * half : (side + 1) * half] = found[e * MOST : (e + 1) * MOST]
                return carry

            lax.fori_loop(0, size // TOK, place, 0, unroll=2)
    outs = []
    for e in range(EXP):
        copy = pltpu.make_async_copy(rows.at[e], rows_out.at[e], out_sems.at[e])
        copy.start()
        outs.append(copy)
    load.wait()
    tile = 256
    for e in range(EXP):

        def multiply(number, carry, e=e):
            columns = pl.ds(pl.multiple_of(number * tile, tile), tile)
            product = jnp.dot(
                scaled[e], rows[e, :, columns], preferred_element_type=jnp.float32
            ).astype(jnp.bfloat16)
            for part in range(2):
                go[e, part, :, columns] = product[part * SHARE : (part + 1) * SHARE]
                stay[e, part, :, columns] = product[(part + 2) * SHARE : (part + 3) * SHARE]
            return carry

        lax.fori_loop(0, width // tile, multiply, 0)
        for part in range(2):
            for kind, (source, target) in enumerate(((go, go_out), (stay, stay_out))):
                copy = pltpu.make_async_copy(
                    source.at[e, part], target.at[part, e], out_sems.at[2 + (e * 2 + part) * 2 + kind]
                )
                copy.start()
                outs.append(copy)
    for copy in outs:
        copy.wait()


def select(order, pick, scaled, pieces):
    half = pieces[0].shape[1]
    width = 2 * half
    anywhere = pl.BlockSpec(memory_space=pl.ANY)
    vmem = pl.BlockSpec(memory_space=pltpu.VMEM)
    smem = pl.BlockSpec(memory_space=pltpu.SMEM)
    shared = (EXP, 2, SHARE, width)
    need = (2 * SOURCES * TOK * half + EXP * CAP * width + EXP * HID * CAP + 2 * EXP * HID * width // 2) * 2
    return pl.pallas_call(
        functools.partial(select_kernel, width),
        in_specs=[smem, vmem, anywhere] + [anywhere] * 10,
        out_specs=[anywhere] * 3,
        out_shape=[
            jax.ShapeDtypeStruct((EXP, CAP, width), jnp.bfloat16),
            jax.ShapeDtypeStruct((2, EXP, SHARE, width), jnp.bfloat16),
            jax.ShapeDtypeStruct((2, EXP, SHARE, width), jnp.bfloat16),
        ],
        scratch_shapes=[
            pltpu.VMEM((2, SOURCES * TOK, half), jnp.bfloat16),
            pltpu.VMEM((EXP, CAP, width), jnp.bfloat16),
            pltpu.VMEM((EXP, HID, CAP), jnp.bfloat16),
            pltpu.VMEM(shared, jnp.bfloat16),
            pltpu.VMEM(shared, jnp.bfloat16),
            pltpu.SemaphoreType.DMA((11,)),
            pltpu.SemaphoreType.DMA((10,)),
        ],
        compiler_params=pltpu.CompilerParams(vmem_limit_bytes=need + 8 * MIB),
        cost_estimate=pl.CostEstimate(
            flops=2 * EXP * CAP * HID * width * 2,
            bytes_accessed=SOURCES * TOK * width * 2 + EXP * CAP * width * 2 + 8 * 10**6,
            transcendentals=0,
        ),
        name="select",
    )(order, pick, scaled, *pieces)


ROW_TILE = 512


def upstream_kernel(has_total, last, first_column, *refs):
    refs = list(refs)
    rows_ref, weight_hbm = refs[0], refs[1]
    weight, sems = refs[-2:]
    expert = pl.program_id(0)
    columns = pl.ds(first_column, weight.shape[2])

    def load(e):
        return pltpu.make_async_copy(weight_hbm.at[e, :, columns], weight.at[e], sems.at[e])

    for e in range(EXP):

        @pl.when((expert == 0) & (pl.program_id(1) == 0))
        def _(e=e):
            load(e).start()

    for e in range(EXP):

        @pl.when((expert == e) & (pl.program_id(1) == 0))
        def _(e=e):
            load(e).wait()

    product = lax.dot_general(
        rows_ref[0], weight[expert], (((1,), (1,)), ((), ())), preferred_element_type=jnp.float32
    )
    at = 2
    if has_total:
        total_ref = refs[at]
        at += 1
    if not last:
        out_ref = refs[at]
        out_ref[0] = product + total_ref[0] if has_total else product
        return
    product = product + total_ref[0]
    padded_ref, gate_ref, pick_ref, hidden_ref, sum_ref = refs[at : at + 5]
    gate = gate_ref[0]
    hidden_ref[0] = (product * jnp.concatenate([gate] * (HID // TOK), axis=1)).astype(jnp.bfloat16)
    sums = jnp.sum(product * padded_ref[0].astype(jnp.float32), axis=1, keepdims=True)
    spread = jnp.where(pick_ref[0].astype(jnp.float32) > 0, sums, 0.0)
    sum_ref[0] = jnp.sum(spread.reshape(ROW_TILE_LAST // MOST, MOST, TOK), axis=1)


ROW_TILE_LAST = 384


def upstream(rows, weight, first_column, total, extra, last):
    width = rows.shape[2]
    tile = ROW_TILE_LAST if last else ROW_TILE
    in_specs = [
        pl.BlockSpec((1, tile, width), lambda e, t: (e, t, 0)),
        pl.BlockSpec(memory_space=pl.ANY),
    ]
    args = [rows, weight]
    total_spec = pl.BlockSpec((1, tile, HID), lambda e, t: (e, t, 0))
    narrow = pl.BlockSpec((1, tile, TOK), lambda e, t: (e, t, 0))
    aliases = {}
    if total is not None:
        in_specs.append(total_spec)
        args.append(total)
        if not last:
            aliases = {2: 0}
    if last:
        in_specs += [total_spec, narrow, narrow]
        args += list(extra)
        out_specs = [
            total_spec,
            pl.BlockSpec((1, tile // MOST, TOK), lambda e, t: (e, t, 0)),
        ]
        out_shape = [
            jax.ShapeDtypeStruct((EXP, CAP, HID), jnp.bfloat16),
            jax.ShapeDtypeStruct((EXP, SOURCES, TOK), jnp.float32),
        ]
    else:
        out_specs = total_spec
        out_shape = jax.ShapeDtypeStruct((EXP, CAP, HID), jnp.float32)
    return pl.pallas_call(
        functools.partial(upstream_kernel, total is not None, last, first_column),
        grid=(EXP, CAP // tile),
        in_specs=in_specs,
        out_specs=out_specs,
        out_shape=out_shape,
        scratch_shapes=[
            pltpu.VMEM((EXP, HID, width), jnp.bfloat16),
            pltpu.SemaphoreType.DMA((EXP,)),
        ],
        input_output_aliases=aliases,
        compiler_params=pltpu.CompilerParams(vmem_limit_bytes=32 * MIB),
        cost_estimate=pl.CostEstimate(
            flops=2 * EXP * CAP * HID * width // 64,
            bytes_accessed=EXP * CAP * HID,
            transcendentals=0,
        ),
        name="finish" if last else "upstream",
    )(*args)


def order_kernel(base_ref, lead_ref, count_ref, hidden_ref, out_ref):
    expert = pl.program_id(0)
    out_ref[...] = jnp.zeros_like(out_ref)

    def one(source, carry):
        at = source * EXP + expert
        column = lax.broadcasted_iota(jnp.int32, (WINDOW, MOST), 1)
        row = lax.broadcasted_iota(jnp.int32, (WINDOW, MOST), 0)
        take = (row == column + lead_ref[at]) & (column < count_ref[at])
        found = jnp.dot(
            jnp.where(take, 1.0, 0.0).astype(jnp.bfloat16),
            hidden_ref[0, pl.ds(pl.multiple_of(source * MOST, MOST), MOST), :],
            preferred_element_type=jnp.float32,
        ).astype(jnp.bfloat16)
        low = pl.multiple_of(base_ref[at], 16)
        out_ref[0, 0, pl.ds(low, WINDOW), :] += found
        return carry

    lax.fori_loop(0, SOURCES, one, 0, unroll=2)


def in_slot_order(base, lead, count, hidden):
    return pl.pallas_call(
        order_kernel,
        grid_spec=pltpu.PrefetchScalarGridSpec(
            num_scalar_prefetch=3,
            grid=(EXP,),
            in_specs=[pl.BlockSpec((1, CAP, HID), lambda e, *_: (e, 0, 0))],
            out_specs=pl.BlockSpec((1, 1, CAP, HID), lambda e, *_: (0, e, 0, 0)),
        ),
        out_shape=jax.ShapeDtypeStruct((1, EXP, CAP, HID), jnp.bfloat16),
        compiler_params=pltpu.CompilerParams(vmem_limit_bytes=24 * MIB),
        cost_estimate=pl.CostEstimate(flops=10**9, bytes_accessed=12 * 10**6, transcendentals=0),
        name="in_slot_order",
    )(base, lead, count, hidden)


def ring_first(block, up, down):
    return send(block, up), send(block, down)


def ring_second(from_up, from_down, up, down):
    half = from_up.shape[0] // 2
    return send(from_up[:half], up), send(from_down[half:], down)


def gate_tables(gates, index):
    index_t = index[0].T
    gates_t = gates[0].T
    experts = jnp.arange(SOURCES * EXP, dtype=jnp.int32)[None, :, None]
    dense = jnp.sum(
        jnp.where(index_t[:, None, :] == experts, gates_t[:, None, :].astype(jnp.float32), 0.0), axis=0
    )
    dense = dense.astype(jnp.bfloat16).reshape(SOURCES, EXP, TOK)
    gate = lax.all_to_all(dense, "expert", split_axis=0, concat_axis=0, tiled=True)
    present = gate > 0
    ones = present.astype(jnp.float32)
    earlier_token = jnp.triu(jnp.ones((TOK, TOK), jnp.float32), 1)
    rank = jnp.einsum("set,tu->seu", ones, earlier_token, preferred_element_type=jnp.float32)
    counts = jnp.sum(ones, axis=2)
    earlier_source = jnp.tril(jnp.ones((SOURCES, SOURCES), jnp.float32), -1)
    offset = jnp.einsum("rs,se->re", earlier_source, counts, preferred_element_type=jnp.float32)
    offset = offset.astype(jnp.int32)
    base = jnp.minimum(offset // 16 * 16, CAP - WINDOW)
    rank = jnp.where(present, rank.astype(jnp.int32), -1)
    flat = (SOURCES * EXP,)
    return (
        gate.astype(jnp.float32),
        rank,
        base.reshape(flat),
        (offset - base).reshape(flat),
        counts.astype(jnp.int32).reshape(flat),
    )


def body(out_grad, gates, expert_index, saved_hidden, down_weight):
    tokens = out_grad[0]
    order = lax.dynamic_index_in_dim(
        jnp.asarray(source_orders()), lax.axis_index("expert"), 0, keepdims=False
    )
    replica = lax.axis_index("replica")
    place = jnp.stack([replica % 2, replica // 2]).astype(jnp.int32)

    count = len(STAGES)
    starts = [sum(STAGES[:s]) for s in range(count)]

    def first_swap(group, hold):
        lefts, rights, spans = [], [], []
        at = 0
        for s in group:
            half = STAGES[s] // 2
            lefts.append(tokens[:, starts[s] : starts[s] + half])
            rights.append(tokens[:, starts[s] + half : starts[s] + 2 * half])
            spans.append((at, at + half))
            at += half
        mine = jnp.concatenate(lefts + rights, axis=1)
        if hold is not None:
            mine = after(mine, *hold)
        met = send(mine, X_SWAP)
        return jnp.concatenate([mine, met], axis=0), at, spans, group, met

    def first_rings(swapped, ready):
        both, at, spans, group, _ = swapped
        if ready is not None:
            both = after(both, ready)
        a, b = both[:, :at], both[:, at:]
        a_up, a_down = ring_first(a, Z_UP, Z_DOWN)
        b_up, b_down = ring_first(b, Y_UP, Y_DOWN)
        a_far = ring_second(a_up, a_down, Z_UP, Z_DOWN)
        b_far = ring_second(b_up, b_down, Y_UP, Y_DOWN)
        pieces = (a, a_up, a_down, *a_far, b, b_up, b_down, *b_far)
        joined = join(pieces, tuple(spans))
        return {s: joined[2 * i : 2 * i + 2] for i, s in enumerate(group)}

    swapped = first_swap(GROUPS[0], None)
    gate, rank, base, lead, counts = gate_tables(after(gates, swapped[4]), expert_index)
    wide = first_rings(swapped, None)
    swapped = first_swap(GROUPS[1], (wide[0][0],))
    scaled, padded, row_gate, pick = prepare(
        base, lead, counts, place, after(rank, wide[0][0]), gate, saved_hidden
    )
    total = None
    shares = []
    near = pair = None
    selected, crossed = [], []
    hidden = sums = None

    def second_ring_first(s):
        a, b = wide[s]
        hold = list(near or ())
        if s >= 2:
            hold.append(selected[s - 2])
        if hold:
            a, b = after(a, *hold), after(b, *hold)
        return (a, b), (*ring_first(a, Y_UP, Y_DOWN), *ring_first(b, Z_UP, Z_DOWN))

    def second_ring_second(near, hold):
        ends = [after(value, *hold) if hold else value for value in near]
        return (
            ring_second(ends[0], ends[1], Y_UP, Y_DOWN),
            ring_second(ends[2], ends[3], Z_UP, Z_DOWN),
        )

    (a, b), near = second_ring_first(0)
    wide.update(first_rings(swapped, scaled))
    far_a, far_b = second_ring_second(near, ())
    for s in range(count):
        pieces = (a, near[0], near[1], *far_a, b, near[2], near[3], *far_b)
        last = s + 1 == count
        if not last:
            (a, b), near = second_ring_first(s + 1)
        hold = []
        if s > 0:
            hold += [total, pair]
        lag = CROSSED_LAG if last else 1
        if s >= lag:
            hold.append(crossed[s - lag])
        if s + 1 < count:
            hold += [a, b]
        if hold:
            pieces = tuple(after(piece, *hold) for piece in pieces)
        rows, go, stay = select(order, pick, scaled, pieces)
        selected.append(go)
        leaving = after(go, *near) if not last else go
        met = lax.ppermute(leaving, "replica", CORE_SWAP)
        pair = (met.astype(jnp.float32) + stay.astype(jnp.float32)).astype(jnp.bfloat16)
        across = lax.ppermute(pair[1], "replica", XHI_SWAP)
        shares.append(
            (pair[0].astype(jnp.float32) + across.astype(jnp.float32)).astype(jnp.bfloat16)
        )
        if not last:
            far_a, far_b = second_ring_second(near, (go,))
        if last:
            rows = after(rows, pair)
        crossed.append(across)
        result = upstream(rows, down_weight, starts[s], total, (padded, row_gate, pick), last)
        if last:
            hidden, sums = result
        else:
            total = result

    weight_grad = jnp.concatenate(shares, axis=2)
    back = lax.all_to_all(
        jnp.swapaxes(sums, 0, 1), "expert", split_axis=0, concat_axis=0, tiled=True
    ).reshape(SOURCES * EXP, TOK)
    hidden_grad = in_slot_order(base, lead, counts, hidden)
    index_t = expert_index[0].T
    experts = jnp.arange(SOURCES * EXP, dtype=jnp.int32)[None, :, None]
    picked = jnp.sum(jnp.where(index_t[:, None, :] == experts, back[None], 0.0), axis=1)
    gate_grad = picked.T[None]
    return (hidden_grad, gate_grad, weight_grad)


def solution(mesh):
    in_specs = (
        P("replica", "expert", None),
        P("replica", "expert", None),
        P("replica", "expert", None),
        P("replica", "expert", None, None),
        P("expert", None, None),
    )
    out_specs = (
        P("replica", "expert", None, None),
        P("replica", "expert", None),
        P("expert", "replica", None),
    )
    return jax.shard_map(body, mesh=mesh, in_specs=in_specs, out_specs=out_specs, check_vma=False)
```

```python
import functools

import jax
import jax.numpy as jnp
import numpy as np
from jax import lax
from jax.experimental import pallas as pl
from jax.experimental.pallas import tpu as pltpu
from jax.sharding import PartitionSpec as P

SOURCES = 32
TOK = 128
HID = 768
CAP = 1536
EXP = 2
MOST = 48
PICK = EXP * MOST
WINDOW = 64
SHARE = HID // 4
STAGES = (2304, 1792)
MIB = 1024 * 1024
CROSSED_LAG = 1
LIMIT_HALVE = 60

NZ, NX, NY = 4, 2, 4


def index_of(z, x, y):
    return ((z % NZ) * NX + (x % NX)) * NY + (y % NY)


def shift(dz, dx, dy):
    return [
        (index_of(z, x, y), index_of(z + dz, x + dx, y + dy))
        for z in range(NZ)
        for x in range(NX)
        for y in range(NY)
    ]


Y_UP, Y_DOWN = shift(0, 0, 1), shift(0, 0, -1)
Z_UP, Z_DOWN = shift(1, 0, 0), shift(-1, 0, 0)
X_SWAP = shift(0, 1, 0)
CORE_SWAP = [(0, 1), (1, 0), (2, 3), (3, 2)]
XHI_SWAP = [(0, 2), (2, 0), (1, 3), (3, 1)]

RING = (0, -1, 1, 2)


def send(value, pairs):
    return lax.ppermute(value, "expert", pairs)


def after(value, *others):
    return lax.optimization_barrier((value, *others))[0]


def source_orders():
    table = np.zeros((SOURCES, 2 * SOURCES), np.int32)
    for z in range(NZ):
        for x in range(NX):
            for y in range(NY):
                row = []
                for first_z in (True, False):
                    for outer in RING:
                        for inner in RING:
                            for dx in range(NX):
                                dz, dy = (inner, outer) if first_z else (outer, inner)
                                row.append(index_of(z + dz, x + dx, y + dy))
                table[index_of(z, x, y)] = row
    return table


def prepare_kernel(
    base_ref, lead_ref, count_ref, place_ref, rank_ref, gate_ref, saved_ref,
    scaled_ref, padded_ref, row_gate_ref, pick_ref, moved,
):
    expert = pl.program_id(0)

    def one(source, carry):
        rank = rank_ref[source, pl.ds(expert, 1), :]
        gate = gate_ref[source, pl.ds(expert, 1), :]
        at = source * EXP + expert
        rows = pl.ds(pl.multiple_of(source * MOST, MOST), MOST)
        hit = lax.broadcasted_iota(jnp.int32, (MOST, TOK), 0) == rank
        pick_ref[0, rows, :] = jnp.where(hit, 1.0, 0.0).astype(jnp.bfloat16)
        row_gate = jnp.sum(jnp.where(hit, gate, 0.0), axis=1, keepdims=True)
        row_gate_ref[0, rows, :] = jnp.broadcast_to(row_gate, (MOST, TOK))
        window = saved_ref[0, 0, pl.ds(pl.multiple_of(base_ref[at], 16), WINDOW), :]
        row = lax.broadcasted_iota(jnp.int32, (MOST, WINDOW), 0)
        column = lax.broadcasted_iota(jnp.int32, (MOST, WINDOW), 1)
        take = (column == row + lead_ref[at]) & (row < count_ref[at])
        found = jnp.dot(
            jnp.where(take, 1.0, 0.0).astype(jnp.bfloat16), window,
            preferred_element_type=jnp.float32,
        )
        padded_ref[0, rows, :] = found.astype(jnp.bfloat16)
        moved[rows, :] = found * row_gate
        return carry

    lax.fori_loop(0, SOURCES, one, 0)
    core, xhi = place_ref[0], place_ref[1]
    step = 256

    def turn(tile, carry):
        rows = pl.ds(pl.multiple_of(tile * step, step), step)
        turned = moved[rows, :].T.astype(jnp.bfloat16)
        for owner in range(4):
            owner_xhi, owner_core = owner // 2, owner % 2
            block = jnp.where(core == owner_core, 2, 0) + jnp.where(xhi == owner_xhi, 0, 1)
            start = pl.multiple_of(block * SHARE, SHARE)
            scaled_ref[0, pl.ds(start, SHARE), rows] = turned[owner * SHARE : (owner + 1) * SHARE, :]
        return carry

    lax.fori_loop(0, CAP // step, turn, 0)


def prepare(base, lead, count, place, rank, gate, saved):
    table = pl.BlockSpec((SOURCES, EXP, TOK), lambda e, *_: (0, 0, 0))
    return pl.pallas_call(
        prepare_kernel,
        grid_spec=pltpu.PrefetchScalarGridSpec(
            num_scalar_prefetch=4,
            grid=(EXP,),
            in_specs=[table, table, pl.BlockSpec((1, 1, CAP, HID), lambda e, *_: (0, e, 0, 0))],
            out_specs=[
                pl.BlockSpec((1, HID, CAP), lambda e, *_: (e, 0, 0)),
                pl.BlockSpec((1, CAP, HID), lambda e, *_: (e, 0, 0)),
                pl.BlockSpec((1, CAP, TOK), lambda e, *_: (e, 0, 0)),
                pl.BlockSpec((1, CAP, TOK), lambda e, *_: (e, 0, 0)),
            ],
            scratch_shapes=[pltpu.VMEM((CAP, HID), jnp.float32)],
        ),
        out_shape=[
            jax.ShapeDtypeStruct((EXP, HID, CAP), jnp.bfloat16),
            jax.ShapeDtypeStruct((EXP, CAP, HID), jnp.bfloat16),
            jax.ShapeDtypeStruct((EXP, CAP, TOK), jnp.float32),
            jax.ShapeDtypeStruct((EXP, CAP, TOK), jnp.bfloat16),
        ],
        compiler_params=pltpu.CompilerParams(vmem_limit_bytes=60 * MIB),
        cost_estimate=pl.CostEstimate(flops=10**9, bytes_accessed=16 * 10**6, transcendentals=0),
        name="prepare",
    )(base, lead, count, place, rank, gate, saved)


def join_kernel(spans, staged, *refs):
    pieces, outs = refs[:16], refs[16 : 16 + 2 * len(spans)]
    rest = refs[16 + 2 * len(spans) :]
    sems = rest[-1]
    targets = rest[: len(outs)] if staged else outs
    groups = []
    for number, (low, high) in enumerate(spans):
        for side in range(2):
            first = 0
            group = []
            for part in range(8):
                piece = pieces[side * 8 + part]
                size = piece.shape[0]
                copy = pltpu.make_async_copy(
                    piece.at[:, pl.ds(low, high - low)],
                    targets[number * 2 + side].at[pl.ds(first, size), :],
                    sems.at[len(groups) * 8 + part],
                )
                copy.start()
                group.append(copy)
                first += size
            groups.append(group)
    leaving = []
    for number, group in enumerate(groups):
        for copy in group:
            copy.wait()
        if staged:
            copy = pltpu.make_async_copy(
                targets[number], outs[number], sems.at[8 * len(groups) + number]
            )
            copy.start()
            leaving.append(copy)
    for copy in leaving:
        copy.wait()


def join(pieces, spans, staged):
    shapes = []
    for low, high in spans:
        shapes += [(1024, high - low)] * 2
    place = pl.BlockSpec(memory_space=pl.ANY if staged else pltpu.VMEM)
    return pl.pallas_call(
        functools.partial(join_kernel, spans, staged),
        in_specs=[pl.BlockSpec(memory_space=pl.ANY)] * 16,
        out_specs=[place] * len(shapes),
        out_shape=[jax.ShapeDtypeStruct(shape, jnp.bfloat16) for shape in shapes],
        scratch_shapes=[pltpu.VMEM(shape, jnp.bfloat16) for shape in shapes if staged]
        + [pltpu.SemaphoreType.DMA((9 * len(shapes),))],
        compiler_params=pltpu.CompilerParams(vmem_limit_bytes=16 * MIB),
        cost_estimate=pl.CostEstimate(flops=0, bytes_accessed=2 * MIB, transcendentals=0),
        name="join",
    )(*pieces)


def halve_kernel(*refs):
    values, outs, held, sems = refs[:4], refs[4:8], refs[8], refs[9]
    size = held.shape[1]
    copies = []
    for i in range(4):
        copy = pltpu.make_async_copy(
            values[i].at[pl.ds((i % 2) * size, size), :], held.at[i], sems.at[i]
        )
        copy.start()
        copies.append(copy)
    leaving = []
    for i in range(4):
        copies[i].wait()
        copy = pltpu.make_async_copy(held.at[i], outs[i], sems.at[4 + i])
        copy.start()
        leaving.append(copy)
    for copy in leaving:
        copy.wait()


def halve(values):
    rows, width = values[0].shape
    anywhere = pl.BlockSpec(memory_space=pl.ANY)
    return pl.pallas_call(
        halve_kernel,
        in_specs=[anywhere] * 4,
        out_specs=[anywhere] * 4,
        out_shape=[jax.ShapeDtypeStruct((rows // 2, width), jnp.bfloat16)] * 4,
        scratch_shapes=[
            pltpu.VMEM((4, rows // 2, width), jnp.bfloat16),
            pltpu.SemaphoreType.DMA((8,)),
        ],
        compiler_params=pltpu.CompilerParams(vmem_limit_bytes=LIMIT_HALVE * MIB),
        cost_estimate=pl.CostEstimate(flops=0, bytes_accessed=2 * MIB, transcendentals=0),
        name="halve",
    )(*values)


def select_kernel(width, order_ref, pick_ref, scaled_hbm, *refs):
    pieces = refs[:10]
    rows_out, go_out, stay_out = refs[10:13]
    taken, rows, scaled, go, stay, in_sems, out_sems = refs[13:]
    half = width // 2
    copies = []
    for side in range(2):
        first = 0
        for number in range(5):
            piece = pieces[side * 5 + number]
            size = piece.shape[0]
            copy = pltpu.make_async_copy(
                piece, taken.at[side, pl.ds(first, size), :], in_sems.at[side * 5 + number]
            )
            copy.start()
            copies.append((copy, first, size))
            first += size
    load = pltpu.make_async_copy(scaled_hbm, scaled, in_sems.at[10])
    load.start()

    for side in range(2):
        for number in range(5):
            copy, first, size = copies[side * 5 + number]
            copy.wait()

            def place(block, carry, side=side, first=first):
                at = first // TOK + block
                source = order_ref[side * SOURCES + at]
                to = pl.ds(pl.multiple_of(source * MOST, MOST), MOST)
                pick = jnp.concatenate([pick_ref[e, to, :] for e in range(EXP)], axis=0)
                start = pl.multiple_of(at * TOK, TOK)
                found = jnp.dot(
                    pick, taken[side, pl.ds(start, TOK), :], preferred_element_type=jnp.float32
                ).astype(jnp.bfloat16)
                for e in range(EXP):
                    rows[e, to, side * half : (side + 1) * half] = found[e * MOST : (e + 1) * MOST]
                return carry

            lax.fori_loop(0, size // TOK, place, 0, unroll=2)
    outs = []
    for e in range(EXP):
        copy = pltpu.make_async_copy(rows.at[e], rows_out.at[e], out_sems.at[e])
        copy.start()
        outs.append(copy)
    load.wait()
    tile = 256
    for e in range(EXP):

        def multiply(number, carry, e=e):
            columns = pl.ds(pl.multiple_of(number * tile, tile), tile)
            product = jnp.dot(
                scaled[e], rows[e, :, columns], preferred_element_type=jnp.float32
            ).astype(jnp.bfloat16)
            for part in range(2):
                go[e, part, :, columns] = product[part * SHARE : (part + 1) * SHARE]
                stay[e, part, :, columns] = product[(part + 2) * SHARE : (part + 3) * SHARE]
            return carry

        lax.fori_loop(0, width // tile, multiply, 0)
        for part in range(2):
            for kind, (source, target) in enumerate(((go, go_out), (stay, stay_out))):
                copy = pltpu.make_async_copy(
                    source.at[e, part], target.at[part, e], out_sems.at[2 + (e * 2 + part) * 2 + kind]
                )
                copy.start()
                outs.append(copy)
    for copy in outs:
        copy.wait()


def select(order, pick, scaled, pieces):
    half = pieces[0].shape[1]
    width = 2 * half
    anywhere = pl.BlockSpec(memory_space=pl.ANY)
    vmem = pl.BlockSpec(memory_space=pltpu.VMEM)
    smem = pl.BlockSpec(memory_space=pltpu.SMEM)
    shared = (EXP, 2, SHARE, width)
    need = (2 * SOURCES * TOK * half + EXP * CAP * width + EXP * HID * CAP + 2 * EXP * HID * width // 2) * 2
    return pl.pallas_call(
        functools.partial(select_kernel, width),
        in_specs=[smem, vmem, anywhere] + [anywhere] * 10,
        out_specs=[anywhere] * 3,
        out_shape=[
            jax.ShapeDtypeStruct((EXP, CAP, width), jnp.bfloat16),
            jax.ShapeDtypeStruct((2, EXP, SHARE, width), jnp.bfloat16),
            jax.ShapeDtypeStruct((2, EXP, SHARE, width), jnp.bfloat16),
        ],
        scratch_shapes=[
            pltpu.VMEM((2, SOURCES * TOK, half), jnp.bfloat16),
            pltpu.VMEM((EXP, CAP, width), jnp.bfloat16),
            pltpu.VMEM((EXP, HID, CAP), jnp.bfloat16),
            pltpu.VMEM(shared, jnp.bfloat16),
            pltpu.VMEM(shared, jnp.bfloat16),
            pltpu.SemaphoreType.DMA((11,)),
            pltpu.SemaphoreType.DMA((10,)),
        ],
        compiler_params=pltpu.CompilerParams(vmem_limit_bytes=60 * MIB),
        cost_estimate=pl.CostEstimate(
            flops=2 * EXP * CAP * HID * width * 2,
            bytes_accessed=SOURCES * TOK * width * 2 + EXP * CAP * width * 2 + 8 * 10**6,
            transcendentals=0,
        ),
        name="select",
    )(order, pick, scaled, *pieces)


ROW_TILE = 512


def upstream_kernel(has_total, last, first_column, *refs):
    refs = list(refs)
    rows_ref, weight_hbm = refs[0], refs[1]
    weight, sems = refs[-2:]
    expert = pl.program_id(0)
    columns = pl.ds(first_column, weight.shape[2])

    def load(e):
        return pltpu.make_async_copy(weight_hbm.at[e, :, columns], weight.at[e], sems.at[e])

    for e in range(EXP):

        @pl.when((expert == 0) & (pl.program_id(1) == 0))
        def _(e=e):
            load(e).start()

    for e in range(EXP):

        @pl.when((expert == e) & (pl.program_id(1) == 0))
        def _(e=e):
            load(e).wait()

    product = lax.dot_general(
        rows_ref[0], weight[expert], (((1,), (1,)), ((), ())), preferred_element_type=jnp.float32
    )
    at = 2
    if has_total:
        total_ref = refs[at]
        at += 1
    if not last:
        out_ref = refs[at]
        out_ref[0] = product + total_ref[0] if has_total else product
        return
    product = product + total_ref[0]
    padded_ref, gate_ref, pick_ref, hidden_ref, sum_ref = refs[at : at + 5]
    gate = gate_ref[0]
    hidden_ref[0] = (product * jnp.concatenate([gate] * (HID // TOK), axis=1)).astype(jnp.bfloat16)
    sums = jnp.sum(product * padded_ref[0].astype(jnp.float32), axis=1, keepdims=True)
    spread = jnp.where(pick_ref[0].astype(jnp.float32) > 0, sums, 0.0)
    sum_ref[0] = jnp.sum(spread.reshape(ROW_TILE_LAST // MOST, MOST, TOK), axis=1)


ROW_TILE_LAST = 384


def upstream(rows, weight, first_column, total, extra, last):
    width = rows.shape[2]
    tile = ROW_TILE_LAST if last else ROW_TILE
    in_specs = [
        pl.BlockSpec((1, tile, width), lambda e, t: (e, t, 0)),
        pl.BlockSpec(memory_space=pl.ANY),
    ]
    args = [rows, weight]
    total_spec = pl.BlockSpec((1, tile, HID), lambda e, t: (e, t, 0))
    narrow = pl.BlockSpec((1, tile, TOK), lambda e, t: (e, t, 0))
    aliases = {}
    if total is not None:
        in_specs.append(total_spec)
        args.append(total)
        if not last:
            aliases = {2: 0}
    if last:
        in_specs += [total_spec, narrow, narrow]
        args += list(extra)
        out_specs = [
            total_spec,
            pl.BlockSpec((1, tile // MOST, TOK), lambda e, t: (e, t, 0)),
        ]
        out_shape = [
            jax.ShapeDtypeStruct((EXP, CAP, HID), jnp.bfloat16),
            jax.ShapeDtypeStruct((EXP, SOURCES, TOK), jnp.float32),
        ]
    else:
        out_specs = total_spec
        out_shape = jax.ShapeDtypeStruct((EXP, CAP, HID), jnp.float32)
    return pl.pallas_call(
        functools.partial(upstream_kernel, total is not None, last, first_column),
        grid=(EXP, CAP // tile),
        in_specs=in_specs,
        out_specs=out_specs,
        out_shape=out_shape,
        scratch_shapes=[
            pltpu.VMEM((EXP, HID, width), jnp.bfloat16),
            pltpu.SemaphoreType.DMA((EXP,)),
        ],
        input_output_aliases=aliases,
        compiler_params=pltpu.CompilerParams(vmem_limit_bytes=60 * MIB),
        cost_estimate=pl.CostEstimate(
            flops=2 * EXP * CAP * HID * width // 64,
            bytes_accessed=EXP * CAP * HID,
            transcendentals=0,
        ),
        name="finish" if last else "upstream",
    )(*args)


def order_kernel(base_ref, lead_ref, count_ref, hidden_ref, out_ref):
    expert = pl.program_id(0)
    out_ref[...] = jnp.zeros_like(out_ref)

    def one(source, carry):
        at = source * EXP + expert
        column = lax.broadcasted_iota(jnp.int32, (WINDOW, MOST), 1)
        row = lax.broadcasted_iota(jnp.int32, (WINDOW, MOST), 0)
        take = (row == column + lead_ref[at]) & (column < count_ref[at])
        found = jnp.dot(
            jnp.where(take, 1.0, 0.0).astype(jnp.bfloat16),
            hidden_ref[0, pl.ds(pl.multiple_of(source * MOST, MOST), MOST), :],
            preferred_element_type=jnp.float32,
        ).astype(jnp.bfloat16)
        low = pl.multiple_of(base_ref[at], 16)
        out_ref[0, 0, pl.ds(low, WINDOW), :] += found
        return carry

    lax.fori_loop(0, SOURCES, one, 0, unroll=2)


def in_slot_order(base, lead, count, hidden):
    return pl.pallas_call(
        order_kernel,
        grid_spec=pltpu.PrefetchScalarGridSpec(
            num_scalar_prefetch=3,
            grid=(EXP,),
            in_specs=[pl.BlockSpec((1, CAP, HID), lambda e, *_: (e, 0, 0))],
            out_specs=pl.BlockSpec((1, 1, CAP, HID), lambda e, *_: (0, e, 0, 0)),
        ),
        out_shape=jax.ShapeDtypeStruct((1, EXP, CAP, HID), jnp.bfloat16),
        compiler_params=pltpu.CompilerParams(vmem_limit_bytes=60 * MIB),
        cost_estimate=pl.CostEstimate(flops=10**9, bytes_accessed=12 * 10**6, transcendentals=0),
        name="in_slot_order",
    )(base, lead, count, hidden)


def ring_first(block, up, down):
    return send(block, up), send(block, down)


def ring_second(ends, up, down):
    return send(ends[0], up), send(ends[1], down)


def send_gates(gates, index):
    index_t = index[0].T
    gates_t = gates[0].T
    experts = jnp.arange(SOURCES * EXP, dtype=jnp.int32)[None, :, None]
    dense = jnp.sum(
        jnp.where(index_t[:, None, :] == experts, gates_t[:, None, :].astype(jnp.float32), 0.0), axis=0
    )
    dense = dense.astype(jnp.bfloat16).reshape(SOURCES, EXP, TOK)
    return lax.all_to_all(dense, "expert", split_axis=0, concat_axis=0, tiled=True)


def gate_tables(gate):
    present = gate > 0
    ones = present.astype(jnp.float32)
    earlier_token = jnp.triu(jnp.ones((TOK, TOK), jnp.float32), 1)
    rank = jnp.einsum("set,tu->seu", ones, earlier_token, preferred_element_type=jnp.float32)
    counts = jnp.sum(ones, axis=2)
    earlier_source = jnp.tril(jnp.ones((SOURCES, SOURCES), jnp.float32), -1)
    offset = jnp.einsum("rs,se->re", earlier_source, counts, preferred_element_type=jnp.float32)
    offset = offset.astype(jnp.int32)
    base = jnp.minimum(offset // 16 * 16, CAP - WINDOW)
    rank = jnp.where(present, rank.astype(jnp.int32), -1)
    flat = (SOURCES * EXP,)
    return (
        gate.astype(jnp.float32),
        rank,
        base.reshape(flat),
        (offset - base).reshape(flat),
        counts.astype(jnp.int32).reshape(flat),
    )


def body(out_grad, gates, expert_index, saved_hidden, down_weight):
    tokens = out_grad[0]
    order = lax.dynamic_index_in_dim(
        jnp.asarray(source_orders()), lax.axis_index("expert"), 0, keepdims=False
    )
    replica = lax.axis_index("replica")
    place = jnp.stack([replica % 2, replica // 2]).astype(jnp.int32)

    count = len(STAGES)
    starts = [sum(STAGES[:s]) for s in range(count)]

    halves = [width // 2 for width in STAGES]
    spans = [(sum(halves[:s]), sum(halves[: s + 1])) for s in range(count)]

    def split(rows):
        lefts = [rows[:, starts[s] : starts[s] + halves[s]] for s in range(count)]
        rights = [rows[:, starts[s] + halves[s] : starts[s] + STAGES[s]] for s in range(count)]
        return jnp.concatenate(lefts, axis=1), jnp.concatenate(rights, axis=1)

    met = send(tokens, X_SWAP)
    sides = []
    mine = split(tokens)
    links = ((Z_UP, Z_DOWN), (Y_UP, Y_DOWN))
    own_near = [ring_first(block, *link) for block, link in zip(mine, links)]
    own_far = [send(near[0], link[0]) for near, link in zip(own_near, links)]
    other = split(met)
    other_near = [ring_first(block, *link) for block, link in zip(other, links)]
    other_far = [send(near[1], link[1]) for near, link in zip(other_near, links)]
    for side in range(2):
        sides += [mine[side], other[side]]
        for way in range(2):
            sides += [own_near[side][way], other_near[side][way]]
        sides += [own_far[side], other_far[side]]
    gate = send_gates(after(gates, own_near[0][0]), expert_index)
    wide = {0: join([after(piece, gate) for piece in sides], spans[:1], False)}
    joined = join([after(piece, wide[0][0]) for piece in sides], spans[1:], True)
    wide.update({s: joined[2 * s - 2 : 2 * s] for s in range(1, count)})
    gate, rank, base, lead, counts = gate_tables(after(gate, wide[0][0]))
    scaled, padded, row_gate, pick = prepare(
        base, lead, counts, place, after(rank, joined[0]), gate, saved_hidden
    )

    total = None
    shares = []
    near = pair = None
    selected, crossed = [], []
    hidden = sums = None

    def second_ring_first(s):
        a, b = wide[s]
        hold = list(near or ())
        if s >= 2:
            hold.append(selected[s - 2])
        if hold:
            a, b = after(a, *hold), after(b, *hold)
        return (a, b), (*ring_first(a, Y_UP, Y_DOWN), *ring_first(b, Z_UP, Z_DOWN))

    def second_ring_second(near, hold):
        ends = [after(value, *hold) if hold else value for value in near]
        ends = halve(ends)
        return ring_second(ends[:2], Y_UP, Y_DOWN), ring_second(ends[2:], Z_UP, Z_DOWN), ends

    (a, b), near = second_ring_first(0)
    far_a, far_b, _ = second_ring_second(near, (scaled,))
    for s in range(count):
        pieces = (a, near[0], near[1], *far_a, b, near[2], near[3], *far_b)
        last = s + 1 == count
        if not last:
            (a, b), near = second_ring_first(s + 1)
        hold = []
        if s > 0:
            hold += [total, pair]
        lag = CROSSED_LAG if last else 1
        if s >= lag:
            hold.append(crossed[s - lag])
        if s + 1 < count:
            hold += [a, b]
        if hold:
            pieces = tuple(after(piece, *hold) for piece in pieces)
        rows, go, stay = select(order, pick, scaled, pieces)
        selected.append(go)
        leaving = after(go, *near) if not last else go
        met = lax.ppermute(leaving, "replica", CORE_SWAP)
        if not last:
            next_far_a, next_far_b, ends = second_ring_second(near, (go,))
        cuts = (0, STAGES[s]) if last else (0, STAGES[s] // 2, STAGES[s])
        parts = []
        for low, high in zip(cuts, cuts[1:]):
            pair = (
                met[1, :, :, low:high].astype(jnp.float32)
                + stay[1, :, :, low:high].astype(jnp.float32)
            ).astype(jnp.bfloat16)
            across = lax.ppermute(after(pair, *parts), "replica", XHI_SWAP)
            if not parts:
                crossed.append(across)
            parts.append(across)
        shares.append((met[0], stay[0], parts))
        if not last:
            far_a, far_b = next_far_a, next_far_b
        if last:
            rows = after(rows, pair)
        result = upstream(rows, down_weight, starts[s], total, (padded, row_gate, pick), last)
        if last:
            hidden, sums = result
        else:
            total = result

    finished = []
    for s, (met, stay, parts) in enumerate(shares):
        parts = [after(part, sums) for part in parts] if s + 1 < count else parts
        across = jnp.concatenate(parts, axis=2).astype(jnp.float32)
        pair = met.astype(jnp.float32) + stay.astype(jnp.float32)
        finished.append((pair + across).astype(jnp.bfloat16))
    weight_grad = jnp.concatenate(finished, axis=2)
    back = lax.all_to_all(
        jnp.swapaxes(sums, 0, 1), "expert", split_axis=0, concat_axis=0, tiled=True
    ).reshape(SOURCES * EXP, TOK)
    hidden_grad = in_slot_order(base, lead, counts, hidden)
    index_t = expert_index[0].T
    experts = jnp.arange(SOURCES * EXP, dtype=jnp.int32)[None, :, None]
    picked = jnp.sum(jnp.where(index_t[:, None, :] == experts, back[None], 0.0), axis=1)
    gate_grad = picked.T[None]
    return (hidden_grad, gate_grad, weight_grad)


def solution(mesh):
    in_specs = (
        P("replica", "expert", None),
        P("replica", "expert", None),
        P("replica", "expert", None),
        P("replica", "expert", None, None),
        P("expert", None, None),
    )
    out_specs = (
        P("replica", "expert", None, None),
        P("replica", "expert", None),
        P("expert", "replica", None),
    )
    return jax.shard_map(body, mesh=mesh, in_specs=in_specs, out_specs=out_specs, check_vma=False)
```

```python
import functools

import jax
import jax.numpy as jnp
import numpy as np
from jax import lax
from jax.experimental import pallas as pl
from jax.experimental.pallas import tpu as pltpu
from jax.sharding import PartitionSpec as P

SOURCES = 32
TOK = 128
HID = 768
CAP = 1536
EXP = 2
MOST = 48
PICK = EXP * MOST
WINDOW = 64
SHARE = HID // 4
STAGES = (2304, 1792)
MIB = 1024 * 1024
CROSSED_LAG = 1
LIMIT_HALVE = 60

NZ, NX, NY = 4, 2, 4


def index_of(z, x, y):
    return ((z % NZ) * NX + (x % NX)) * NY + (y % NY)


def shift(dz, dx, dy):
    return [
        (index_of(z, x, y), index_of(z + dz, x + dx, y + dy))
        for z in range(NZ)
        for x in range(NX)
        for y in range(NY)
    ]


Y_UP, Y_DOWN = shift(0, 0, 1), shift(0, 0, -1)
Z_UP, Z_DOWN = shift(1, 0, 0), shift(-1, 0, 0)
X_SWAP = shift(0, 1, 0)
CORE_SWAP = [(0, 1), (1, 0), (2, 3), (3, 2)]
XHI_SWAP = [(0, 2), (2, 0), (1, 3), (3, 1)]

RING = (0, -1, 1, 2)


def send(value, pairs):
    return lax.ppermute(value, "expert", pairs)


def after(value, *others):
    return lax.optimization_barrier((value, *others))[0]


def source_orders():
    table = np.zeros((SOURCES, 2 * SOURCES), np.int32)
    for z in range(NZ):
        for x in range(NX):
            for y in range(NY):
                row = []
                for first_z in (True, False):
                    for outer in RING:
                        for inner in RING:
                            for dx in range(NX):
                                dz, dy = (inner, outer) if first_z else (outer, inner)
                                row.append(index_of(z + dz, x + dx, y + dy))
                table[index_of(z, x, y)] = row
    return table


def prepare_kernel(
    base_ref, lead_ref, count_ref, place_ref, rank_ref, gate_ref, saved_ref,
    scaled_ref, padded_ref, row_gate_ref, pick_ref, moved,
):
    expert = pl.program_id(0)

    def one(source, carry):
        rank = rank_ref[source, pl.ds(expert, 1), :]
        gate = gate_ref[source, pl.ds(expert, 1), :]
        at = source * EXP + expert
        rows = pl.ds(pl.multiple_of(source * MOST, MOST), MOST)
        hit = lax.broadcasted_iota(jnp.int32, (MOST, TOK), 0) == rank
        pick_ref[0, rows, :] = jnp.where(hit, 1.0, 0.0).astype(jnp.bfloat16)
        row_gate = jnp.sum(jnp.where(hit, gate, 0.0), axis=1, keepdims=True)
        row_gate_ref[0, rows, :] = jnp.broadcast_to(row_gate, (MOST, TOK))
        window = saved_ref[0, 0, pl.ds(pl.multiple_of(base_ref[at], 16), WINDOW), :]
        row = lax.broadcasted_iota(jnp.int32, (MOST, WINDOW), 0)
        column = lax.broadcasted_iota(jnp.int32, (MOST, WINDOW), 1)
        take = (column == row + lead_ref[at]) & (row < count_ref[at])
        found = jnp.dot(
            jnp.where(take, 1.0, 0.0).astype(jnp.bfloat16), window,
            preferred_element_type=jnp.float32,
        )
        padded_ref[0, rows, :] = found.astype(jnp.bfloat16)
        moved[rows, :] = found * row_gate
        return carry

    lax.fori_loop(0, SOURCES, one, 0)
    core, xhi = place_ref[0], place_ref[1]
    step = 256

    def turn(tile, carry):
        rows = pl.ds(pl.multiple_of(tile * step, step), step)
        turned = moved[rows, :].T.astype(jnp.bfloat16)
        for owner in range(4):
            owner_xhi, owner_core = owner // 2, owner % 2
            block = jnp.where(core == owner_core, 2, 0) + jnp.where(xhi == owner_xhi, 0, 1)
            start = pl.multiple_of(block * SHARE, SHARE)
            scaled_ref[0, pl.ds(start, SHARE), rows] = turned[owner * SHARE : (owner + 1) * SHARE, :]
        return carry

    lax.fori_loop(0, CAP // step, turn, 0)


def prepare(base, lead, count, place, rank, gate, saved):
    table = pl.BlockSpec((SOURCES, EXP, TOK), lambda e, *_: (0, 0, 0))
    return pl.pallas_call(
        prepare_kernel,
        grid_spec=pltpu.PrefetchScalarGridSpec(
            num_scalar_prefetch=4,
            grid=(EXP,),
            in_specs=[table, table, pl.BlockSpec((1, 1, CAP, HID), lambda e, *_: (0, e, 0, 0))],
            out_specs=[
                pl.BlockSpec((1, HID, CAP), lambda e, *_: (e, 0, 0)),
                pl.BlockSpec((1, CAP, HID), lambda e, *_: (e, 0, 0)),
                pl.BlockSpec((1, CAP, TOK), lambda e, *_: (e, 0, 0)),
                pl.BlockSpec((1, CAP, TOK), lambda e, *_: (e, 0, 0)),
            ],
            scratch_shapes=[pltpu.VMEM((CAP, HID), jnp.float32)],
        ),
        out_shape=[
            jax.ShapeDtypeStruct((EXP, HID, CAP), jnp.bfloat16),
            jax.ShapeDtypeStruct((EXP, CAP, HID), jnp.bfloat16),
            jax.ShapeDtypeStruct((EXP, CAP, TOK), jnp.float32),
            jax.ShapeDtypeStruct((EXP, CAP, TOK), jnp.bfloat16),
        ],
        compiler_params=pltpu.CompilerParams(vmem_limit_bytes=60 * MIB),
        cost_estimate=pl.CostEstimate(flops=10**9, bytes_accessed=16 * 10**6, transcendentals=0),
        name="prepare",
    )(base, lead, count, place, rank, gate, saved)


def join_kernel(spans, staged, *refs):
    pieces, outs = refs[:16], refs[16 : 16 + 2 * len(spans)]
    rest = refs[16 + 2 * len(spans) :]
    sems = rest[-1]
    targets = rest[: len(outs)] if staged else outs
    groups = []
    for number, (low, high) in enumerate(spans):
        for side in range(2):
            first = 0
            group = []
            for part in range(8):
                piece = pieces[side * 8 + part]
                size = piece.shape[0]
                copy = pltpu.make_async_copy(
                    piece.at[:, pl.ds(low, high - low)],
                    targets[number * 2 + side].at[pl.ds(first, size), :],
                    sems.at[len(groups) * 8 + part],
                )
                copy.start()
                group.append(copy)
                first += size
            groups.append(group)
    leaving = []
    for number, group in enumerate(groups):
        for copy in group:
            copy.wait()
        if staged:
            copy = pltpu.make_async_copy(
                targets[number], outs[number], sems.at[8 * len(groups) + number]
            )
            copy.start()
            leaving.append(copy)
    for copy in leaving:
        copy.wait()


def join(pieces, spans, staged):
    shapes = []
    for low, high in spans:
        shapes += [(1024, high - low)] * 2
    place = pl.BlockSpec(memory_space=pl.ANY if staged else pltpu.VMEM)
    return pl.pallas_call(
        functools.partial(join_kernel, spans, staged),
        in_specs=[pl.BlockSpec(memory_space=pl.ANY)] * 16,
        out_specs=[place] * len(shapes),
        out_shape=[jax.ShapeDtypeStruct(shape, jnp.bfloat16) for shape in shapes],
        scratch_shapes=[pltpu.VMEM(shape, jnp.bfloat16) for shape in shapes if staged]
        + [pltpu.SemaphoreType.DMA((9 * len(shapes),))],
        compiler_params=pltpu.CompilerParams(vmem_limit_bytes=16 * MIB),
        cost_estimate=pl.CostEstimate(flops=0, bytes_accessed=2 * MIB, transcendentals=0),
        name="join",
    )(*pieces)


def halve_kernel(*refs):
    values, outs, held, sems = refs[:4], refs[4:8], refs[8], refs[9]
    size = held.shape[1]
    copies = []
    for i in range(4):
        copy = pltpu.make_async_copy(
            values[i].at[pl.ds((i % 2) * size, size), :], held.at[i], sems.at[i]
        )
        copy.start()
        copies.append(copy)
    leaving = []
    for i in range(4):
        copies[i].wait()
        copy = pltpu.make_async_copy(held.at[i], outs[i], sems.at[4 + i])
        copy.start()
        leaving.append(copy)
    for copy in leaving:
        copy.wait()


def halve(values):
    rows, width = values[0].shape
    anywhere = pl.BlockSpec(memory_space=pl.ANY)
    return pl.pallas_call(
        halve_kernel,
        in_specs=[anywhere] * 4,
        out_specs=[anywhere] * 4,
        out_shape=[jax.ShapeDtypeStruct((rows // 2, width), jnp.bfloat16)] * 4,
        scratch_shapes=[
            pltpu.VMEM((4, rows // 2, width), jnp.bfloat16),
            pltpu.SemaphoreType.DMA((8,)),
        ],
        compiler_params=pltpu.CompilerParams(vmem_limit_bytes=LIMIT_HALVE * MIB),
        cost_estimate=pl.CostEstimate(flops=0, bytes_accessed=2 * MIB, transcendentals=0),
        name="halve",
    )(*values)


def select_kernel(width, order_ref, pick_ref, scaled_hbm, *refs):
    pieces = refs[:10]
    rows_out, go_out, stay_out = refs[10:13]
    taken, rows, scaled, go, stay, in_sems, out_sems = refs[13:]
    half = width // 2
    copies = []
    for side in range(2):
        first = 0
        for number in range(5):
            piece = pieces[side * 5 + number]
            size = piece.shape[0]
            copy = pltpu.make_async_copy(
                piece, taken.at[side, pl.ds(first, size), :], in_sems.at[side * 5 + number]
            )
            copy.start()
            copies.append((copy, first, size))
            first += size
    load = pltpu.make_async_copy(scaled_hbm, scaled, in_sems.at[10])
    load.start()

    for side in range(2):
        for number in range(5):
            copy, first, size = copies[side * 5 + number]
            copy.wait()

            def place(block, carry, side=side, first=first):
                at = first // TOK + block
                source = order_ref[side * SOURCES + at]
                to = pl.ds(pl.multiple_of(source * MOST, MOST), MOST)
                pick = jnp.concatenate([pick_ref[e, to, :] for e in range(EXP)], axis=0)
                start = pl.multiple_of(at * TOK, TOK)
                found = jnp.dot(
                    pick, taken[side, pl.ds(start, TOK), :], preferred_element_type=jnp.float32
                ).astype(jnp.bfloat16)
                for e in range(EXP):
                    rows[e, to, side * half : (side + 1) * half] = found[e * MOST : (e + 1) * MOST]
                return carry

            lax.fori_loop(0, size // TOK, place, 0, unroll=4)
    outs = []
    for e in range(EXP):
        copy = pltpu.make_async_copy(rows.at[e], rows_out.at[e], out_sems.at[e])
        copy.start()
        outs.append(copy)
    load.wait()
    tile = width // 3 if width % 768 == 0 else width // 2
    for e in range(EXP):

        def multiply(number, carry, e=e):
            columns = pl.ds(pl.multiple_of(number * tile, tile), tile)
            product = jnp.dot(
                scaled[e], rows[e, :, columns], preferred_element_type=jnp.float32
            ).astype(jnp.bfloat16)
            for part in range(2):
                go[e, part, :, columns] = product[part * SHARE : (part + 1) * SHARE]
                stay[e, part, :, columns] = product[(part + 2) * SHARE : (part + 3) * SHARE]
            return carry

        lax.fori_loop(0, width // tile, multiply, 0)
        for part in range(2):
            for kind, (source, target) in enumerate(((go, go_out), (stay, stay_out))):
                copy = pltpu.make_async_copy(
                    source.at[e, part], target.at[part, e], out_sems.at[2 + (e * 2 + part) * 2 + kind]
                )
                copy.start()
                outs.append(copy)
    for copy in outs:
        copy.wait()


def select(order, pick, scaled, pieces):
    half = pieces[0].shape[1]
    width = 2 * half
    anywhere = pl.BlockSpec(memory_space=pl.ANY)
    vmem = pl.BlockSpec(memory_space=pltpu.VMEM)
    smem = pl.BlockSpec(memory_space=pltpu.SMEM)
    shared = (EXP, 2, SHARE, width)
    need = (2 * SOURCES * TOK * half + EXP * CAP * width + EXP * HID * CAP + 2 * EXP * HID * width // 2) * 2
    return pl.pallas_call(
        functools.partial(select_kernel, width),
        in_specs=[smem, vmem, anywhere] + [anywhere] * 10,
        out_specs=[anywhere] * 3,
        out_shape=[
            jax.ShapeDtypeStruct((EXP, CAP, width), jnp.bfloat16),
            jax.ShapeDtypeStruct((2, EXP, SHARE, width), jnp.bfloat16),
            jax.ShapeDtypeStruct((2, EXP, SHARE, width), jnp.bfloat16),
        ],
        scratch_shapes=[
            pltpu.VMEM((2, SOURCES * TOK, half), jnp.bfloat16),
            pltpu.VMEM((EXP, CAP, width), jnp.bfloat16),
            pltpu.VMEM((EXP, HID, CAP), jnp.bfloat16),
            pltpu.VMEM(shared, jnp.bfloat16),
            pltpu.VMEM(shared, jnp.bfloat16),
            pltpu.SemaphoreType.DMA((11,)),
            pltpu.SemaphoreType.DMA((10,)),
        ],
        compiler_params=pltpu.CompilerParams(vmem_limit_bytes=60 * MIB),
        cost_estimate=pl.CostEstimate(
            flops=2 * EXP * CAP * HID * width * 2,
            bytes_accessed=SOURCES * TOK * width * 2 + EXP * CAP * width * 2 + 8 * 10**6,
            transcendentals=0,
        ),
        name="select",
    )(order, pick, scaled, *pieces)


ROW_TILE = 512


def upstream_kernel(has_total, last, first_column, *refs):
    refs = list(refs)
    rows_ref, weight_hbm = refs[0], refs[1]
    weight, sems = refs[-2:]
    expert = pl.program_id(0)
    columns = pl.ds(first_column, weight.shape[2])

    def load(e):
        return pltpu.make_async_copy(weight_hbm.at[e, :, columns], weight.at[e], sems.at[e])

    for e in range(EXP):

        @pl.when((expert == 0) & (pl.program_id(1) == 0))
        def _(e=e):
            load(e).start()

    for e in range(EXP):

        @pl.when((expert == e) & (pl.program_id(1) == 0))
        def _(e=e):
            load(e).wait()

    product = lax.dot_general(
        rows_ref[0], weight[expert], (((1,), (1,)), ((), ())), preferred_element_type=jnp.float32
    )
    at = 2
    if has_total:
        total_ref = refs[at]
        at += 1
    if not last:
        out_ref = refs[at]
        out_ref[0] = product + total_ref[0] if has_total else product
        return
    product = product + total_ref[0]
    padded_ref, gate_ref, pick_ref, hidden_ref, sum_ref = refs[at : at + 5]
    gate = gate_ref[0]
    hidden_ref[0] = (product * jnp.concatenate([gate] * (HID // TOK), axis=1)).astype(jnp.bfloat16)
    sums = jnp.sum(product * padded_ref[0].astype(jnp.float32), axis=1, keepdims=True)
    spread = jnp.where(pick_ref[0].astype(jnp.float32) > 0, sums, 0.0)
    sum_ref[0] = jnp.sum(spread.reshape(ROW_TILE_LAST // MOST, MOST, TOK), axis=1)


ROW_TILE_LAST = 768


def upstream(rows, weight, first_column, total, extra, last):
    width = rows.shape[2]
    tile = ROW_TILE_LAST if last else ROW_TILE
    in_specs = [
        pl.BlockSpec((1, tile, width), lambda e, t: (e, t, 0)),
        pl.BlockSpec(memory_space=pl.ANY),
    ]
    args = [rows, weight]
    total_spec = pl.BlockSpec((1, tile, HID), lambda e, t: (e, t, 0))
    narrow = pl.BlockSpec((1, tile, TOK), lambda e, t: (e, t, 0))
    aliases = {}
    if total is not None:
        in_specs.append(total_spec)
        args.append(total)
        if not last:
            aliases = {2: 0}
    if last:
        in_specs += [total_spec, narrow, narrow]
        args += list(extra)
        out_specs = [
            total_spec,
            pl.BlockSpec((1, tile // MOST, TOK), lambda e, t: (e, t, 0)),
        ]
        out_shape = [
            jax.ShapeDtypeStruct((EXP, CAP, HID), jnp.bfloat16),
            jax.ShapeDtypeStruct((EXP, SOURCES, TOK), jnp.float32),
        ]
    else:
        out_specs = total_spec
        out_shape = jax.ShapeDtypeStruct((EXP, CAP, HID), jnp.float32)
    return pl.pallas_call(
        functools.partial(upstream_kernel, total is not None, last, first_column),
        grid=(EXP, CAP // tile),
        in_specs=in_specs,
        out_specs=out_specs,
        out_shape=out_shape,
        scratch_shapes=[
            pltpu.VMEM((EXP, HID, width), jnp.bfloat16),
            pltpu.SemaphoreType.DMA((EXP,)),
        ],
        input_output_aliases=aliases,
        compiler_params=pltpu.CompilerParams(vmem_limit_bytes=60 * MIB),
        cost_estimate=pl.CostEstimate(
            flops=2 * EXP * CAP * HID * width // 64,
            bytes_accessed=EXP * CAP * HID,
            transcendentals=0,
        ),
        name="finish" if last else "upstream",
    )(*args)


def order_kernel(base_ref, lead_ref, count_ref, hidden_ref, out_ref):
    expert = pl.program_id(0)
    out_ref[...] = jnp.zeros_like(out_ref)

    def one(source, carry):
        at = source * EXP + expert
        column = lax.broadcasted_iota(jnp.int32, (WINDOW, MOST), 1)
        row = lax.broadcasted_iota(jnp.int32, (WINDOW, MOST), 0)
        take = (row == column + lead_ref[at]) & (column < count_ref[at])
        found = jnp.dot(
            jnp.where(take, 1.0, 0.0).astype(jnp.bfloat16),
            hidden_ref[0, pl.ds(pl.multiple_of(source * MOST, MOST), MOST), :],
            preferred_element_type=jnp.float32,
        ).astype(jnp.bfloat16)
        low = pl.multiple_of(base_ref[at], 16)
        out_ref[0, 0, pl.ds(low, WINDOW), :] += found
        return carry

    lax.fori_loop(0, SOURCES, one, 0, unroll=2)


def in_slot_order(base, lead, count, hidden):
    return pl.pallas_call(
        order_kernel,
        grid_spec=pltpu.PrefetchScalarGridSpec(
            num_scalar_prefetch=3,
            grid=(EXP,),
            in_specs=[pl.BlockSpec((1, CAP, HID), lambda e, *_: (e, 0, 0))],
            out_specs=pl.BlockSpec((1, 1, CAP, HID), lambda e, *_: (0, e, 0, 0)),
        ),
        out_shape=jax.ShapeDtypeStruct((1, EXP, CAP, HID), jnp.bfloat16),
        compiler_params=pltpu.CompilerParams(vmem_limit_bytes=60 * MIB),
        cost_estimate=pl.CostEstimate(flops=10**9, bytes_accessed=12 * 10**6, transcendentals=0),
        name="in_slot_order",
    )(base, lead, count, hidden)


def ring_first(block, up, down):
    return send(block, up), send(block, down)


def ring_second(ends, up, down):
    return send(ends[0], up), send(ends[1], down)


def send_gates(gates, index):
    index_t = index[0].T
    gates_t = gates[0].T
    experts = jnp.arange(SOURCES * EXP, dtype=jnp.int32)[None, :, None]
    dense = jnp.sum(
        jnp.where(index_t[:, None, :] == experts, gates_t[:, None, :].astype(jnp.float32), 0.0), axis=0
    )
    dense = dense.astype(jnp.bfloat16).reshape(SOURCES, EXP, TOK)
    return lax.all_to_all(dense, "expert", split_axis=0, concat_axis=0, tiled=True)


def gate_tables(gate):
    present = gate > 0
    ones = present.astype(jnp.float32)
    earlier_token = jnp.triu(jnp.ones((TOK, TOK), jnp.float32), 1)
    rank = jnp.einsum("set,tu->seu", ones, earlier_token, preferred_element_type=jnp.float32)
    counts = jnp.sum(ones, axis=2)
    earlier_source = jnp.tril(jnp.ones((SOURCES, SOURCES), jnp.float32), -1)
    offset = jnp.einsum("rs,se->re", earlier_source, counts, preferred_element_type=jnp.float32)
    offset = offset.astype(jnp.int32)
    base = jnp.minimum(offset // 16 * 16, CAP - WINDOW)
    rank = jnp.where(present, rank.astype(jnp.int32), -1)
    flat = (SOURCES * EXP,)
    return (
        gate.astype(jnp.float32),
        rank,
        base.reshape(flat),
        (offset - base).reshape(flat),
        counts.astype(jnp.int32).reshape(flat),
    )


def body(out_grad, gates, expert_index, saved_hidden, down_weight):
    tokens = out_grad[0]
    order = lax.dynamic_index_in_dim(
        jnp.asarray(source_orders()), lax.axis_index("expert"), 0, keepdims=False
    )
    replica = lax.axis_index("replica")
    place = jnp.stack([replica % 2, replica // 2]).astype(jnp.int32)

    count = len(STAGES)
    starts = [sum(STAGES[:s]) for s in range(count)]

    halves = [width // 2 for width in STAGES]
    spans = [(sum(halves[:s]), sum(halves[: s + 1])) for s in range(count)]

    def split(rows):
        lefts = [rows[:, starts[s] : starts[s] + halves[s]] for s in range(count)]
        rights = [rows[:, starts[s] + halves[s] : starts[s] + STAGES[s]] for s in range(count)]
        return jnp.concatenate(lefts, axis=1), jnp.concatenate(rights, axis=1)

    met = send(tokens, X_SWAP)
    sides = []
    mine = split(tokens)
    links = ((Z_UP, Z_DOWN), (Y_UP, Y_DOWN))
    own_near = [ring_first(block, *link) for block, link in zip(mine, links)]
    own_far = [send(near[0], link[0]) for near, link in zip(own_near, links)]
    other = split(met)
    other_near = [ring_first(block, *link) for block, link in zip(other, links)]
    other_far = [send(near[1], link[1]) for near, link in zip(other_near, links)]
    for side in range(2):
        sides += [mine[side], other[side]]
        for way in range(2):
            sides += [own_near[side][way], other_near[side][way]]
        sides += [own_far[side], other_far[side]]
    gate = send_gates(after(gates, own_near[0][0]), expert_index)
    wide = {0: join([after(piece, gate) for piece in sides], spans[:1], False)}
    joined = join([after(piece, wide[0][0]) for piece in sides], spans[1:], True)
    wide.update({s: joined[2 * s - 2 : 2 * s] for s in range(1, count)})
    gate, rank, base, lead, counts = gate_tables(after(gate, wide[0][0]))
    scaled, padded, row_gate, pick = prepare(
        base, lead, counts, place, after(rank, joined[0]), gate, saved_hidden
    )

    total = None
    shares = []
    near = pair = None
    selected, crossed = [], []
    hidden = sums = None

    def second_ring_first(s):
        a, b = wide[s]
        hold = list(near or ())
        if s >= 2:
            hold.append(selected[s - 2])
        if hold:
            a, b = after(a, *hold), after(b, *hold)
        return (a, b), (*ring_first(a, Y_UP, Y_DOWN), *ring_first(b, Z_UP, Z_DOWN))

    def second_ring_second(near, hold):
        ends = [after(value, *hold) if hold else value for value in near]
        ends = halve(ends)
        return ring_second(ends[:2], Y_UP, Y_DOWN), ring_second(ends[2:], Z_UP, Z_DOWN), ends

    (a, b), near = second_ring_first(0)
    far_a, far_b, _ = second_ring_second(near, (scaled,))
    for s in range(count):
        pieces = (a, near[0], near[1], *far_a, b, near[2], near[3], *far_b)
        last = s + 1 == count
        if not last:
            (a, b), near = second_ring_first(s + 1)
        hold = []
        if s > 0:
            hold += [total, pair]
        lag = CROSSED_LAG if last else 1
        if s >= lag:
            hold.append(crossed[s - lag])
        if s + 1 < count:
            hold += [a, b]
        if hold:
            pieces = tuple(after(piece, *hold) for piece in pieces)
        rows, go, stay = select(order, pick, scaled, pieces)
        selected.append(go)
        leaving = after(go, *near) if not last else go
        met = lax.ppermute(leaving, "replica", CORE_SWAP)
        if not last:
            next_far_a, next_far_b, ends = second_ring_second(near, (go,))
        cuts = (0, STAGES[s]) if last else (0, STAGES[s] // 2, STAGES[s])
        parts = []
        for low, high in zip(cuts, cuts[1:]):
            pair = (
                met[1, :, :, low:high].astype(jnp.float32)
                + stay[1, :, :, low:high].astype(jnp.float32)
            ).astype(jnp.bfloat16)
            across = lax.ppermute(after(pair, *parts), "replica", XHI_SWAP)
            if not parts:
                crossed.append(across)
            parts.append(across)
        shares.append((met[0], stay[0], parts))
        if not last:
            far_a, far_b = next_far_a, next_far_b
        if last:
            rows = after(rows, pair)
        result = upstream(rows, down_weight, starts[s], total, (padded, row_gate, pick), last)
        if last:
            hidden, sums = result
        else:
            total = result

    finished = []
    for s, (met, stay, parts) in enumerate(shares):
        parts = [after(part, sums) for part in parts] if s + 1 < count else parts
        across = jnp.concatenate(parts, axis=2).astype(jnp.float32)
        pair = met.astype(jnp.float32) + stay.astype(jnp.float32)
        finished.append((pair + across).astype(jnp.bfloat16))
    weight_grad = jnp.concatenate(finished, axis=2)
    back = lax.all_to_all(
        jnp.swapaxes(sums, 0, 1), "expert", split_axis=0, concat_axis=0, tiled=True
    ).reshape(SOURCES * EXP, TOK)
    hidden_grad = in_slot_order(base, lead, counts, hidden)
    back = after(back, weight_grad, hidden_grad)
    index_t = expert_index[0].T
    experts = jnp.arange(SOURCES * EXP, dtype=jnp.int32)[None, :, None]
    picked = jnp.sum(jnp.where(index_t[:, None, :] == experts, back[None], 0.0), axis=1)
    gate_grad = picked.T[None]
    return (hidden_grad, gate_grad, weight_grad)


def solution(mesh):
    in_specs = (
        P("replica", "expert", None),
        P("replica", "expert", None),
        P("replica", "expert", None),
        P("replica", "expert", None, None),
        P("expert", None, None),
    )
    out_specs = (
        P("replica", "expert", None, None),
        P("replica", "expert", None),
        P("expert", "replica", None),
    )
    return jax.shard_map(body, mesh=mesh, in_specs=in_specs, out_specs=out_specs, check_vma=False)
```

```python
import functools

import jax
import jax.numpy as jnp
import numpy as np
from jax import lax
from jax.experimental import pallas as pl
from jax.experimental.pallas import tpu as pltpu
from jax.sharding import PartitionSpec as P

SOURCES = 32
TOK = 128
HID = 768
CAP = 1536
EXP = 2
MOST = 48
PICK = EXP * MOST
WINDOW = 64
SHARE = HID // 4
STAGES = (2304, 1792)
MIB = 1024 * 1024
CROSSED_LAG = 1
LIMIT_HALVE = 60

NZ, NX, NY = 4, 2, 4


def index_of(z, x, y):
    return ((z % NZ) * NX + (x % NX)) * NY + (y % NY)


def shift(dz, dx, dy):
    return [
        (index_of(z, x, y), index_of(z + dz, x + dx, y + dy))
        for z in range(NZ)
        for x in range(NX)
        for y in range(NY)
    ]


Y_UP, Y_DOWN = shift(0, 0, 1), shift(0, 0, -1)
Z_UP, Z_DOWN = shift(1, 0, 0), shift(-1, 0, 0)
X_SWAP = shift(0, 1, 0)
CORE_SWAP = [(0, 1), (1, 0), (2, 3), (3, 2)]
XHI_SWAP = [(0, 2), (2, 0), (1, 3), (3, 1)]

RING = (0, -1, 1, 2)


def send(value, pairs):
    return lax.ppermute(value, "expert", pairs)


def after(value, *others):
    return lax.optimization_barrier((value, *others))[0]


def source_orders():
    table = np.zeros((SOURCES, 2 * SOURCES), np.int32)
    for z in range(NZ):
        for x in range(NX):
            for y in range(NY):
                row = []
                for first_z in (True, False):
                    for outer in RING:
                        for inner in RING:
                            for dx in range(NX):
                                dz, dy = (inner, outer) if first_z else (outer, inner)
                                row.append(index_of(z + dz, x + dx, y + dy))
                table[index_of(z, x, y)] = row
    return table


def prepare_kernel(
    base_ref, lead_ref, count_ref, place_ref, rank_ref, gate_ref, saved_ref,
    scaled_ref, padded_ref, row_gate_ref, pick_ref, moved,
):
    expert = pl.program_id(0)

    def one(source, carry):
        rank = rank_ref[source, pl.ds(expert, 1), :]
        gate = gate_ref[source, pl.ds(expert, 1), :]
        at = source * EXP + expert
        rows = pl.ds(pl.multiple_of(source * MOST, MOST), MOST)
        hit = lax.broadcasted_iota(jnp.int32, (MOST, TOK), 0) == rank
        pick_ref[0, rows, :] = jnp.where(hit, 1.0, 0.0).astype(jnp.bfloat16)
        row_gate = jnp.sum(jnp.where(hit, gate, 0.0), axis=1, keepdims=True)
        row_gate_ref[0, rows, :] = jnp.broadcast_to(row_gate, (MOST, TOK))
        window = saved_ref[0, 0, pl.ds(pl.multiple_of(base_ref[at], 16), WINDOW), :]
        row = lax.broadcasted_iota(jnp.int32, (MOST, WINDOW), 0)
        column = lax.broadcasted_iota(jnp.int32, (MOST, WINDOW), 1)
        take = (column == row + lead_ref[at]) & (row < count_ref[at])
        found = jnp.dot(
            jnp.where(take, 1.0, 0.0).astype(jnp.bfloat16), window,
            preferred_element_type=jnp.float32,
        )
        padded_ref[0, rows, :] = found.astype(jnp.bfloat16)
        moved[rows, :] = found * row_gate
        return carry

    lax.fori_loop(0, SOURCES, one, 0)
    core, xhi = place_ref[0], place_ref[1]
    step = 256

    def turn(tile, carry):
        rows = pl.ds(pl.multiple_of(tile * step, step), step)
        turned = moved[rows, :].T.astype(jnp.bfloat16)
        for owner in range(4):
            owner_xhi, owner_core = owner // 2, owner % 2
            block = jnp.where(core == owner_core, 2, 0) + jnp.where(xhi == owner_xhi, 0, 1)
            start = pl.multiple_of(block * SHARE, SHARE)
            scaled_ref[0, pl.ds(start, SHARE), rows] = turned[owner * SHARE : (owner + 1) * SHARE, :]
        return carry

    lax.fori_loop(0, CAP // step, turn, 0)


def prepare(base, lead, count, place, rank, gate, saved):
    table = pl.BlockSpec((SOURCES, EXP, TOK), lambda e, *_: (0, 0, 0))
    return pl.pallas_call(
        prepare_kernel,
        grid_spec=pltpu.PrefetchScalarGridSpec(
            num_scalar_prefetch=4,
            grid=(EXP,),
            in_specs=[table, table, pl.BlockSpec((1, 1, CAP, HID), lambda e, *_: (0, e, 0, 0))],
            out_specs=[
                pl.BlockSpec((1, HID, CAP), lambda e, *_: (e, 0, 0)),
                pl.BlockSpec((1, CAP, HID), lambda e, *_: (e, 0, 0)),
                pl.BlockSpec((1, CAP, TOK), lambda e, *_: (e, 0, 0)),
                pl.BlockSpec((1, CAP, TOK), lambda e, *_: (e, 0, 0)),
            ],
            scratch_shapes=[pltpu.VMEM((CAP, HID), jnp.float32)],
        ),
        out_shape=[
            jax.ShapeDtypeStruct((EXP, HID, CAP), jnp.bfloat16),
            jax.ShapeDtypeStruct((EXP, CAP, HID), jnp.bfloat16),
            jax.ShapeDtypeStruct((EXP, CAP, TOK), jnp.float32),
            jax.ShapeDtypeStruct((EXP, CAP, TOK), jnp.bfloat16),
        ],
        compiler_params=pltpu.CompilerParams(vmem_limit_bytes=60 * MIB),
        cost_estimate=pl.CostEstimate(flops=10**9, bytes_accessed=16 * 10**6, transcendentals=0),
        name="prepare",
    )(base, lead, count, place, rank, gate, saved)


def join_kernel(spans, staged, *refs):
    pieces, outs = refs[:16], refs[16 : 16 + 2 * len(spans)]
    rest = refs[16 + 2 * len(spans) :]
    sems = rest[-1]
    targets = rest[: len(outs)] if staged else outs
    groups = []
    for number, (low, high) in enumerate(spans):
        for side in range(2):
            first = 0
            group = []
            for part in range(8):
                piece = pieces[side * 8 + part]
                size = piece.shape[0]
                copy = pltpu.make_async_copy(
                    piece.at[:, pl.ds(low, high - low)],
                    targets[number * 2 + side].at[pl.ds(first, size), :],
                    sems.at[len(groups) * 8 + part],
                )
                copy.start()
                group.append(copy)
                first += size
            groups.append(group)
    leaving = []
    for number, group in enumerate(groups):
        for copy in group:
            copy.wait()
        if staged:
            copy = pltpu.make_async_copy(
                targets[number], outs[number], sems.at[8 * len(groups) + number]
            )
            copy.start()
            leaving.append(copy)
    for copy in leaving:
        copy.wait()


def join(pieces, spans, staged):
    shapes = []
    for low, high in spans:
        shapes += [(1024, high - low)] * 2
    place = pl.BlockSpec(memory_space=pl.ANY if staged else pltpu.VMEM)
    return pl.pallas_call(
        functools.partial(join_kernel, spans, staged),
        in_specs=[pl.BlockSpec(memory_space=pl.ANY)] * 16,
        out_specs=[place] * len(shapes),
        out_shape=[jax.ShapeDtypeStruct(shape, jnp.bfloat16) for shape in shapes],
        scratch_shapes=[pltpu.VMEM(shape, jnp.bfloat16) for shape in shapes if staged]
        + [pltpu.SemaphoreType.DMA((9 * len(shapes),))],
        compiler_params=pltpu.CompilerParams(vmem_limit_bytes=16 * MIB),
        cost_estimate=pl.CostEstimate(flops=0, bytes_accessed=2 * MIB, transcendentals=0),
        name="join",
    )(*pieces)


def halve_kernel(*refs):
    values, outs, held, sems = refs[:4], refs[4:8], refs[8], refs[9]
    size = held.shape[1]
    copies = []
    for i in range(4):
        copy = pltpu.make_async_copy(
            values[i].at[pl.ds((i % 2) * size, size), :], held.at[i], sems.at[i]
        )
        copy.start()
        copies.append(copy)
    leaving = []
    for i in range(4):
        copies[i].wait()
        copy = pltpu.make_async_copy(held.at[i], outs[i], sems.at[4 + i])
        copy.start()
        leaving.append(copy)
    for copy in leaving:
        copy.wait()


def halve(values):
    rows, width = values[0].shape
    anywhere = pl.BlockSpec(memory_space=pl.ANY)
    return pl.pallas_call(
        halve_kernel,
        in_specs=[anywhere] * 4,
        out_specs=[anywhere] * 4,
        out_shape=[jax.ShapeDtypeStruct((rows // 2, width), jnp.bfloat16)] * 4,
        scratch_shapes=[
            pltpu.VMEM((4, rows // 2, width), jnp.bfloat16),
            pltpu.SemaphoreType.DMA((8,)),
        ],
        compiler_params=pltpu.CompilerParams(vmem_limit_bytes=LIMIT_HALVE * MIB),
        cost_estimate=pl.CostEstimate(flops=0, bytes_accessed=2 * MIB, transcendentals=0),
        name="halve",
    )(*values)


def select_kernel(width, order_ref, pick_ref, scaled_hbm, *refs):
    pieces = refs[:10]
    rows_out, go_out, stay_out = refs[10:13]
    taken, rows, scaled, go, stay, in_sems, out_sems = refs[13:]
    half = width // 2
    copies = []
    for side in range(2):
        first = 0
        for number in range(5):
            piece = pieces[side * 5 + number]
            size = piece.shape[0]
            copy = pltpu.make_async_copy(
                piece, taken.at[side, pl.ds(first, size), :], in_sems.at[side * 5 + number]
            )
            copy.start()
            copies.append((copy, first, size))
            first += size
    load = pltpu.make_async_copy(scaled_hbm, scaled, in_sems.at[10])
    load.start()

    for side in range(2):
        for number in range(5):
            copy, first, size = copies[side * 5 + number]
            copy.wait()

            def place(block, carry, side=side, first=first):
                at = first // TOK + block
                source = order_ref[side * SOURCES + at]
                to = pl.ds(pl.multiple_of(source * MOST, MOST), MOST)
                pick = jnp.concatenate([pick_ref[e, to, :] for e in range(EXP)], axis=0)
                start = pl.multiple_of(at * TOK, TOK)
                found = jnp.dot(
                    pick, taken[side, pl.ds(start, TOK), :], preferred_element_type=jnp.float32
                ).astype(jnp.bfloat16)
                for e in range(EXP):
                    rows[e, to, side * half : (side + 1) * half] = found[e * MOST : (e + 1) * MOST]
                return carry

            lax.fori_loop(0, size // TOK, place, 0, unroll=4)
    outs = []
    for e in range(EXP):
        copy = pltpu.make_async_copy(rows.at[e], rows_out.at[e], out_sems.at[e])
        copy.start()
        outs.append(copy)
    load.wait()
    tile = width // 3 if width % 768 == 0 else width // 2
    for e in range(EXP):

        def multiply(number, carry, e=e):
            columns = pl.ds(pl.multiple_of(number * tile, tile), tile)
            product = jnp.dot(
                scaled[e], rows[e, :, columns], preferred_element_type=jnp.float32
            ).astype(jnp.bfloat16)
            for part in range(2):
                go[e, part, :, columns] = product[part * SHARE : (part + 1) * SHARE]
                stay[e, part, :, columns] = product[(part + 2) * SHARE : (part + 3) * SHARE]
            return carry

        lax.fori_loop(0, width // tile, multiply, 0)
        for part in range(2):
            for kind, (source, target) in enumerate(((go, go_out), (stay, stay_out))):
                copy = pltpu.make_async_copy(
                    source.at[e, part], target.at[part, e], out_sems.at[2 + (e * 2 + part) * 2 + kind]
                )
                copy.start()
                outs.append(copy)
    for copy in outs:
        copy.wait()


def select(order, pick, scaled, pieces):
    half = pieces[0].shape[1]
    width = 2 * half
    anywhere = pl.BlockSpec(memory_space=pl.ANY)
    vmem = pl.BlockSpec(memory_space=pltpu.VMEM)
    smem = pl.BlockSpec(memory_space=pltpu.SMEM)
    shared = (EXP, 2, SHARE, width)
    need = (2 * SOURCES * TOK * half + EXP * CAP * width + EXP * HID * CAP + 2 * EXP * HID * width // 2) * 2
    return pl.pallas_call(
        functools.partial(select_kernel, width),
        in_specs=[smem, vmem, anywhere] + [anywhere] * 10,
        out_specs=[anywhere] * 3,
        out_shape=[
            jax.ShapeDtypeStruct((EXP, CAP, width), jnp.bfloat16),
            jax.ShapeDtypeStruct((2, EXP, SHARE, width), jnp.bfloat16),
            jax.ShapeDtypeStruct((2, EXP, SHARE, width), jnp.bfloat16),
        ],
        scratch_shapes=[
            pltpu.VMEM((2, SOURCES * TOK, half), jnp.bfloat16),
            pltpu.VMEM((EXP, CAP, width), jnp.bfloat16),
            pltpu.VMEM((EXP, HID, CAP), jnp.bfloat16),
            pltpu.VMEM(shared, jnp.bfloat16),
            pltpu.VMEM(shared, jnp.bfloat16),
            pltpu.SemaphoreType.DMA((11,)),
            pltpu.SemaphoreType.DMA((10,)),
        ],
        compiler_params=pltpu.CompilerParams(vmem_limit_bytes=60 * MIB),
        cost_estimate=pl.CostEstimate(
            flops=2 * EXP * CAP * HID * width * 2,
            bytes_accessed=SOURCES * TOK * width * 2 + EXP * CAP * width * 2 + 8 * 10**6,
            transcendentals=0,
        ),
        name="select",
    )(order, pick, scaled, *pieces)


ROW_TILE = 512


def upstream_kernel(has_total, last, first_column, *refs):
    refs = list(refs)
    rows_ref, weight_hbm = refs[0], refs[1]
    weight, sems = refs[-2:]
    expert = pl.program_id(0)
    columns = pl.ds(first_column, weight.shape[2])

    def load(e):
        return pltpu.make_async_copy(weight_hbm.at[e, :, columns], weight.at[e], sems.at[e])

    for e in range(EXP):

        @pl.when((expert == 0) & (pl.program_id(1) == 0))
        def _(e=e):
            load(e).start()

    for e in range(EXP):

        @pl.when((expert == e) & (pl.program_id(1) == 0))
        def _(e=e):
            load(e).wait()

    product = lax.dot_general(
        rows_ref[0], weight[expert], (((1,), (1,)), ((), ())), preferred_element_type=jnp.float32
    )
    at = 2
    if has_total:
        total_ref = refs[at]
        at += 1
    if not last:
        out_ref = refs[at]
        out_ref[0] = product + total_ref[0] if has_total else product
        return
    product = product + total_ref[0]
    padded_ref, gate_ref, pick_ref, hidden_ref, sum_ref = refs[at : at + 5]
    gate = gate_ref[0]
    hidden_ref[0] = (product * jnp.concatenate([gate] * (HID // TOK), axis=1)).astype(jnp.bfloat16)
    sums = jnp.sum(product * padded_ref[0].astype(jnp.float32), axis=1, keepdims=True)
    spread = jnp.where(pick_ref[0].astype(jnp.float32) > 0, sums, 0.0)
    sum_ref[0] = jnp.sum(spread.reshape(ROW_TILE_LAST // MOST, MOST, TOK), axis=1)


ROW_TILE_LAST = 768


def upstream(rows, weight, first_column, total, extra, last):
    width = rows.shape[2]
    tile = ROW_TILE_LAST if last else ROW_TILE
    in_specs = [
        pl.BlockSpec((1, tile, width), lambda e, t: (e, t, 0)),
        pl.BlockSpec(memory_space=pl.ANY),
    ]
    args = [rows, weight]
    total_spec = pl.BlockSpec((1, tile, HID), lambda e, t: (e, t, 0))
    narrow = pl.BlockSpec((1, tile, TOK), lambda e, t: (e, t, 0))
    aliases = {}
    if total is not None:
        in_specs.append(total_spec)
        args.append(total)
        if not last:
            aliases = {2: 0}
    if last:
        in_specs += [total_spec, narrow, narrow]
        args += list(extra)
        out_specs = [
            total_spec,
            pl.BlockSpec((1, tile // MOST, TOK), lambda e, t: (e, t, 0)),
        ]
        out_shape = [
            jax.ShapeDtypeStruct((EXP, CAP, HID), jnp.bfloat16),
            jax.ShapeDtypeStruct((EXP, SOURCES, TOK), jnp.float32),
        ]
    else:
        out_specs = total_spec
        out_shape = jax.ShapeDtypeStruct((EXP, CAP, HID), jnp.float32)
    return pl.pallas_call(
        functools.partial(upstream_kernel, total is not None, last, first_column),
        grid=(EXP, CAP // tile),
        in_specs=in_specs,
        out_specs=out_specs,
        out_shape=out_shape,
        scratch_shapes=[
            pltpu.VMEM((EXP, HID, width), jnp.bfloat16),
            pltpu.SemaphoreType.DMA((EXP,)),
        ],
        input_output_aliases=aliases,
        compiler_params=pltpu.CompilerParams(vmem_limit_bytes=60 * MIB),
        cost_estimate=pl.CostEstimate(
            flops=2 * EXP * CAP * HID * width // 64,
            bytes_accessed=EXP * CAP * HID,
            transcendentals=0,
        ),
        name="finish" if last else "upstream",
    )(*args)


def order_kernel(base_ref, lead_ref, count_ref, hidden_ref, out_ref):
    expert = pl.program_id(0)
    out_ref[...] = jnp.zeros_like(out_ref)

    def one(source, carry):
        at = source * EXP + expert
        column = lax.broadcasted_iota(jnp.int32, (WINDOW, MOST), 1)
        row = lax.broadcasted_iota(jnp.int32, (WINDOW, MOST), 0)
        take = (row == column + lead_ref[at]) & (column < count_ref[at])
        found = jnp.dot(
            jnp.where(take, 1.0, 0.0).astype(jnp.bfloat16),
            hidden_ref[0, pl.ds(pl.multiple_of(source * MOST, MOST), MOST), :],
            preferred_element_type=jnp.float32,
        ).astype(jnp.bfloat16)
        low = pl.multiple_of(base_ref[at], 16)
        out_ref[0, 0, pl.ds(low, WINDOW), :] += found
        return carry

    lax.fori_loop(0, SOURCES, one, 0, unroll=2)


def in_slot_order(base, lead, count, hidden):
    return pl.pallas_call(
        order_kernel,
        grid_spec=pltpu.PrefetchScalarGridSpec(
            num_scalar_prefetch=3,
            grid=(EXP,),
            in_specs=[pl.BlockSpec((1, CAP, HID), lambda e, *_: (e, 0, 0))],
            out_specs=pl.BlockSpec((1, 1, CAP, HID), lambda e, *_: (0, e, 0, 0)),
        ),
        out_shape=jax.ShapeDtypeStruct((1, EXP, CAP, HID), jnp.bfloat16),
        compiler_params=pltpu.CompilerParams(vmem_limit_bytes=60 * MIB),
        cost_estimate=pl.CostEstimate(flops=10**9, bytes_accessed=12 * 10**6, transcendentals=0),
        name="in_slot_order",
    )(base, lead, count, hidden)


def ring_first(block, up, down):
    return send(block, up), send(block, down)


def ring_second(ends, up, down):
    return send(ends[0], up), send(ends[1], down)


def send_gates(gates, index):
    index_t = index[0].T
    gates_t = gates[0].T
    experts = jnp.arange(SOURCES * EXP, dtype=jnp.int32)[None, :, None]
    dense = jnp.sum(
        jnp.where(index_t[:, None, :] == experts, gates_t[:, None, :].astype(jnp.float32), 0.0), axis=0
    )
    dense = dense.astype(jnp.bfloat16).reshape(SOURCES, EXP, TOK)
    return lax.all_to_all(dense, "expert", split_axis=0, concat_axis=0, tiled=True)


def gate_tables(gate):
    present = gate > 0
    ones = present.astype(jnp.float32)
    earlier_token = jnp.triu(jnp.ones((TOK, TOK), jnp.float32), 1)
    rank = jnp.einsum("set,tu->seu", ones, earlier_token, preferred_element_type=jnp.float32)
    counts = jnp.sum(ones, axis=2)
    earlier_source = jnp.tril(jnp.ones((SOURCES, SOURCES), jnp.float32), -1)
    offset = jnp.einsum("rs,se->re", earlier_source, counts, preferred_element_type=jnp.float32)
    offset = offset.astype(jnp.int32)
    base = jnp.minimum(offset // 16 * 16, CAP - WINDOW)
    rank = jnp.where(present, rank.astype(jnp.int32), -1)
    flat = (SOURCES * EXP,)
    return (
        gate.astype(jnp.float32),
        rank,
        base.reshape(flat),
        (offset - base).reshape(flat),
        counts.astype(jnp.int32).reshape(flat),
    )


def body(out_grad, gates, expert_index, saved_hidden, down_weight):
    tokens = out_grad[0]
    order = lax.dynamic_index_in_dim(
        jnp.asarray(source_orders()), lax.axis_index("expert"), 0, keepdims=False
    )
    replica = lax.axis_index("replica")
    place = jnp.stack([replica % 2, replica // 2]).astype(jnp.int32)

    count = len(STAGES)
    starts = [sum(STAGES[:s]) for s in range(count)]

    halves = [width // 2 for width in STAGES]
    spans = [(sum(halves[:s]), sum(halves[: s + 1])) for s in range(count)]

    def split(rows):
        lefts = [rows[:, starts[s] : starts[s] + halves[s]] for s in range(count)]
        rights = [rows[:, starts[s] + halves[s] : starts[s] + STAGES[s]] for s in range(count)]
        return jnp.concatenate(lefts, axis=1), jnp.concatenate(rights, axis=1)

    met = send(tokens, X_SWAP)
    sides = []
    mine = split(tokens)
    links = ((Z_UP, Z_DOWN), (Y_UP, Y_DOWN))
    own_near = [ring_first(block, *link) for block, link in zip(mine, links)]
    own_far = [send(near[0], link[0]) for near, link in zip(own_near, links)]
    other = split(met)
    other_near = [ring_first(block, *link) for block, link in zip(other, links)]
    other_far = [send(near[1], link[1]) for near, link in zip(other_near, links)]
    for side in range(2):
        sides += [mine[side], other[side]]
        for way in range(2):
            sides += [own_near[side][way], other_near[side][way]]
        sides += [own_far[side], other_far[side]]
    gate = send_gates(after(gates, own_near[0][0]), expert_index)
    wide = {0: join([after(piece, gate) for piece in sides], spans[:1], False)}
    joined = join([after(piece, wide[0][0]) for piece in sides], spans[1:], True)
    wide.update({s: joined[2 * s - 2 : 2 * s] for s in range(1, count)})
    gate, rank, base, lead, counts = gate_tables(after(gate, wide[0][0]))
    scaled, padded, row_gate, pick = prepare(
        base, lead, counts, place, after(rank, joined[0]), gate, saved_hidden
    )

    total = None
    shares = []
    near = pair = None
    selected, crossed = [], []
    hidden = sums = None

    def second_ring_first(s):
        a, b = wide[s]
        hold = list(near or ())
        if s >= 2:
            hold.append(selected[s - 2])
        if hold:
            a, b = after(a, *hold), after(b, *hold)
        return (a, b), (*ring_first(a, Y_UP, Y_DOWN), *ring_first(b, Z_UP, Z_DOWN))

    def second_ring_second(near, hold):
        ends = [after(value, *hold) if hold else value for value in near]
        ends = halve(ends)
        return ring_second(ends[:2], Y_UP, Y_DOWN), ring_second(ends[2:], Z_UP, Z_DOWN), ends

    (a, b), near = second_ring_first(0)
    far_a, far_b, _ = second_ring_second(near, (scaled,))
    for s in range(count):
        pieces = (a, near[0], near[1], *far_a, b, near[2], near[3], *far_b)
        last = s + 1 == count
        if not last:
            (a, b), near = second_ring_first(s + 1)
        hold = []
        if s > 0:
            hold += [total, pair]
        lag = CROSSED_LAG if last else 1
        if s >= lag:
            hold.append(crossed[s - lag])
        if s + 1 < count:
            hold += [a, b]
        if hold:
            pieces = tuple(after(piece, *hold) for piece in pieces)
        rows, go, stay = select(order, pick, scaled, pieces)
        selected.append(go)
        leaving = after(go, *near) if not last else go
        met = lax.ppermute(leaving, "replica", CORE_SWAP)
        if not last:
            next_far_a, next_far_b, ends = second_ring_second(near, (go,))
        cuts = (0, STAGES[s]) if last else (0, STAGES[s] // 2, STAGES[s])
        parts = []
        for low, high in zip(cuts, cuts[1:]):
            pair = (
                met[1, :, :, low:high].astype(jnp.float32)
                + stay[1, :, :, low:high].astype(jnp.float32)
            ).astype(jnp.bfloat16)
            across = lax.ppermute(after(pair, *parts), "replica", XHI_SWAP)
            if not parts:
                crossed.append(across)
            parts.append(across)
        shares.append((met[0], stay[0], parts))
        if not last:
            far_a, far_b = next_far_a, next_far_b
        if last:
            rows = after(rows, pair)
        result = upstream(rows, down_weight, starts[s], total, (padded, row_gate, pick), last)
        if last:
            hidden, sums = result
        else:
            total = result

    finished = []
    for s, (met, stay, parts) in enumerate(shares):
        parts = [after(part, sums) for part in parts] if s + 1 < count else parts
        across = jnp.concatenate(parts, axis=2).astype(jnp.float32)
        pair = met.astype(jnp.float32) + stay.astype(jnp.float32)
        finished.append((pair + across).astype(jnp.bfloat16))
    blank = jnp.zeros((EXP, SHARE, STAGES[-1]), jnp.bfloat16)
    weight_grad = after(jnp.concatenate(finished[:-1] + [blank], axis=2), sums)
    weight_grad = lax.dynamic_update_slice(weight_grad, finished[-1], (0, 0, starts[-1]))
    back = lax.all_to_all(
        jnp.swapaxes(sums, 0, 1), "expert", split_axis=0, concat_axis=0, tiled=True
    ).reshape(SOURCES * EXP, TOK)
    hidden_grad = in_slot_order(base, lead, counts, hidden)
    back = after(back, weight_grad, hidden_grad)
    index_t = expert_index[0].T
    experts = jnp.arange(SOURCES * EXP, dtype=jnp.int32)[None, :, None]
    picked = jnp.sum(jnp.where(index_t[:, None, :] == experts, back[None], 0.0), axis=1)
    gate_grad = picked.T[None]
    return (hidden_grad, gate_grad, weight_grad)


def solution(mesh):
    in_specs = (
        P("replica", "expert", None),
        P("replica", "expert", None),
        P("replica", "expert", None),
        P("replica", "expert", None, None),
        P("expert", None, None),
    )
    out_specs = (
        P("replica", "expert", None, None),
        P("replica", "expert", None),
        P("expert", "replica", None),
    )
    return jax.shard_map(body, mesh=mesh, in_specs=in_specs, out_specs=out_specs, check_vma=False)
```
